32 devices in a mesh: blk: 4 (over y, x), grp: 8 (over z, core).
Axes of the slice: x: 2, y: 2, z: 4, core: 2. Of those that a mesh axis runs over, the one named last changes fastest.
Arguments:
- a_blocks: bfloat16 [8, 96, 27, 96, 96], P('grp', 'blk'), may hold values from -0.125 to 0.125
- col_index: int32 [8, 96, 27], P('grp', 'blk'), may hold values from 0 to 95
- prolong: bfloat16 [8, 96, 2, 96, 96], P('grp', 'blk'), may hold values from -0.625 to 0.625
- target: int32 [8, 96, 108], P('grp', 'blk'), may hold values from 0 to 127
Outputs:
- coarse: float32 [8, 16, 96, 96], P('grp', 'blk')
The draws below stay inside these ranges and needn't reach their ends.
All inputs are finite; a program needn't handle non-finite values.
Results may differ from the reference program's by a relative error of at most 0.0029.
Values may be sent and summed in bfloat16 or wider, within the bound.
No kernel may reach another device: no remote copies, remote signals or barrier semaphores. Data moves between devices by JAX's collectives and lax.ppermute only.
A program may use at most 320 MiB of HBM per device.

```python
import math
import jax
import jax.numpy as jnp
from jax import lax

B = 96
KA = 27
KP = 2
FR = 24
GROUPS = 8
FINE_G = 96
COARSE_G = 16


def draw_col_index(key, part):
    shape = (GROUPS, FINE_G, KA)
    key_near = jax.random.fold_in(key, 11)
    key_far = jax.random.fold_in(key, 12)
    key_kind = jax.random.fold_in(key, 13)
    row_ids = jnp.arange(FINE_G, dtype=jnp.int32)[None, :, None]
    offset = jax.random.randint(key_near, shape, -FR, FR + 1, dtype=jnp.int32)
    near_col = jnp.mod(row_ids + offset, FINE_G)
    far_col = jax.random.randint(key_far, shape, 0, FINE_G, dtype=jnp.int32)
    kind = jax.random.randint(key_kind, shape, 0, 5, dtype=jnp.int32)
    return jnp.where(kind == 0, far_col, near_col).astype(jnp.int32)


def draw_target(key, part):
    shape = (GROUPS, FINE_G, KP * KA * KP)
    key_kind = jax.random.fold_in(key, 21)
    key_slot = jax.random.fold_in(key, 22)
    key_far = jax.random.fold_in(key, 23)
    group_ids = jnp.arange(GROUPS, dtype=jnp.int32)[:, None, None]
    kind = jax.random.randint(key_kind, shape, 0, 10, dtype=jnp.int32)
    slot = jax.random.randint(key_slot, shape, 0, COARSE_G, dtype=jnp.int32)
    far_target = jax.random.randint(key_far, shape, 0, GROUPS * COARSE_G, dtype=jnp.int32)
    owner = jnp.where(kind == 1, group_ids - 1, jnp.where(kind == 2, group_ids + 1, group_ids))
    owner = jnp.clip(owner, 0, GROUPS - 1)
    near_target = owner * COARSE_G + slot
    return jnp.where(kind == 0, far_target, near_target).astype(jnp.int32)


def levels(key, extent, pieces, low, high):
    loudness = 1.0
    for axis_at, shards_of in pieces:
        heights = jax.random.uniform(jax.random.fold_in(jax.random.fold_in(key, 6), axis_at), (shards_of,), jnp.float32, low / len(pieces), high / len(pieces))
        loudness = loudness * jnp.repeat(jnp.exp(heights), extent[axis_at] // shards_of).reshape((-1,) + (1,) * (len(extent) - 1 - axis_at))
    return loudness


def gaussian(key, dims, deviation, limit, pieces=(), kind=jnp.bfloat16):
    factor_of = levels(key, dims, pieces, -0.22, 0.18) if pieces else 1.0
    result = jax.random.normal(key, dims, jnp.float32) * deviation * factor_of
    return jnp.minimum(jnp.maximum(result, -limit), limit).astype(kind)


def setup_inputs(seed: int = 0) -> dict:
    seeds = jax.random.split(jax.random.key(seed), 5)
    a_blocks = gaussian(seeds[0], (GROUPS, FINE_G, KA, B, B), (KA * B) ** -0.5, 0.125, ((0, 8), (1, 4)))
    col_index = draw_col_index(jax.random.fold_in(seeds[4], 71), 0)
    prolong = gaussian(seeds[2], (GROUPS, FINE_G, KP, B, B), B ** -0.5, 0.625, ((0, 8), (1, 4)))
    target = draw_target(jax.random.fold_in(seeds[4], 71), 0)
    return {"a_blocks": a_blocks, "col_index": col_index, "prolong": prolong, "target": target}


def reference(a_blocks, col_index, prolong, target):
    slots = GROUPS * COARSE_G
    step = math.gcd(FINE_G, 16)

    def group_term(total, group):
        a_group = a_blocks[group]
        c_group = col_index[group]
        p_group = prolong[group]
        t_group = target[group]

        def rows_term(accum, low):
            a_part = lax.dynamic_slice_in_dim(a_group, low, step, 0).astype(jnp.float32)
            c_part = lax.dynamic_slice_in_dim(c_group, low, step, 0).astype(jnp.int32)
            p_part = lax.dynamic_slice_in_dim(p_group, low, step, 0).astype(jnp.float32)
            t_part = lax.dynamic_slice_in_dim(t_group, low, step, 0).astype(jnp.int32)
            chosen = jnp.take(p_group, c_part, axis=0).astype(jnp.float32)
            product = jnp.einsum("rkab,rkmbc->rkmac", a_part, chosen).astype(jnp.bfloat16)
            product = lax.optimization_barrier(product).astype(jnp.float32)
            partial_value = jnp.einsum("rnba,rkmbc->rnkmac", p_part, product)
            partial_value = partial_value.reshape(-1, B, B)
            accum = accum + jax.ops.segment_sum(partial_value, t_part.reshape(-1), num_segments=slots)
            return accum, None

        starts = jnp.arange(0, FINE_G, step, dtype=jnp.int32)
        total, _ = lax.scan(rows_term, total, starts)
        return total, None

    init = jnp.zeros((slots, B, B), jnp.float32)
    total, _ = lax.scan(group_term, init, jnp.arange(GROUPS, dtype=jnp.int32))
    return total.reshape(GROUPS, COARSE_G, B, B)
```

```python
import functools

import jax
import jax.numpy as jnp
from jax import lax
from jax.experimental import pallas as pl
from jax.experimental.pallas import tpu as pltpu
from jax.sharding import PartitionSpec as P

OWN = 4
UNROLL = 8
RING = 3
LANES = 128
VMEM_LIMIT = 56 * 1024 * 1024


def pack_four(blocks, width):
    strip = LANES - width
    return [
        jnp.concatenate(
            [blocks[t][:, :width], blocks[3][:, strip * t : strip * (t + 1)]], axis=1
        )
        for t in range(3)
    ]


def unpack_last(parts, width):
    return jnp.concatenate([part[:, width:] for part in parts], axis=1)


def pack_kernel(p_ref, out_ref):
    width = p_ref.shape[-1]
    for quad in range(p_ref.shape[0]):
        packed = pack_four([p_ref[quad, t] for t in range(4)], width)
        for t in range(3):
            out_ref[quad, t] = packed[t]


def pack_prolong(prolong):
    width = prolong.shape[-1]
    quads = prolong.shape[1] * prolong.shape[2] // 4
    step = 3
    return pl.pallas_call(
        pack_kernel,
        grid=(quads // step,),
        in_specs=[pl.BlockSpec((step, 4, width, width), lambda g: (g, 0, 0, 0))],
        out_specs=pl.BlockSpec((step, 3, width, LANES), lambda g: (g, 0, 0, 0)),
        out_shape=jax.ShapeDtypeStruct((quads, 3, width, LANES), prolong.dtype),
        name="pack_prolong",
    )(prolong.reshape(quads, 4, width, width))


def work_kernel(cfg, *refs):
    first, last, phase, sources, naccs = (
        cfg["first"], cfg["last"], cfg["phase"], cfg["sources"], cfg["naccs"],
    )
    width, rows, nonzeros, per_row = cfg["width"], cfg["rows"], cfg["nonzeros"], cfg["per_row"]
    slots, members, groups = cfg["slots"], cfg["members"], cfg["groups"]
    quads = rows * per_row // 4
    refs = list(refs)
    take = lambda n: [refs.pop(0) for _ in range(n)]
    list_ref, col_ref, tgt_ref, info_ref = take(4)
    (a_hbm,) = take(1)
    p_hbm = take(sources)
    if not first:
        pt_hbm, acc_in = take(2)
    if last:
        out_refs = take(members)
    else:
        (acc_out,) = take(1)
        if first:
            (pt_out,) = take(1)
    p_vmem, pt, a_buf = take(3)
    accs = take(naccs)
    aps = take(UNROLL)
    a_sem, sem = take(2)

    base = phase * cfg["list_len"]
    turns = info_ref[phase]

    def a_copies(group, slot):
        copies = []
        for u in range(UNROLL):
            v = list_ref[base + group * UNROLL + u]
            i = jnp.minimum(v >> 5, rows - 1)
            copies.append(
                pltpu.make_async_copy(a_hbm.at[i, v & 31], a_buf.at[slot, u], a_sem.at[slot, u])
            )
        return copies

    def start(group, slot):
        for copy in a_copies(group, slot):
            copy.start()

    def wait(slot):
        for u in range(UNROLL):
            pltpu.make_async_copy(a_hbm.at[0, 0], a_buf.at[slot, u], a_sem.at[slot, u]).wait()

    copies = [
        pltpu.make_async_copy(
            p_hbm[s], p_vmem.at[pl.ds(s * quads, quads), pl.ds(0, 3)], sem.at[s]
        )
        for s in range(sources)
    ]
    if not first:
        copies.append(pltpu.make_async_copy(pt_hbm, pt.at[pl.ds(0, rows)], sem.at[sources]))
        copies.append(
            pltpu.make_async_copy(acc_in, accs[0].at[pl.ds(0, slots)], sem.at[sources + 1])
        )
    for copy in copies:
        copy.start()
    for group in range(1, RING):
        start(group, group)

    def clear(s, _):
        for acc in accs if first else accs[1:]:
            acc[s] = jnp.zeros_like(acc[s])
        return 0

    lax.fori_loop(0, slots, clear, 0)
    for copy in copies[: sources]:
        copy.wait()

    def unpack(q, _):
        fourth = unpack_last([p_vmem[q, t] for t in range(3)], width)
        p_vmem[q, 3, :, :width] = fourth
        return 0

    lax.fori_loop(0, sources * quads, unpack, 0)

    if first:

        def transpose(i, _):
            for n in range(per_row):
                block = p_vmem[i // 2, (i % 2) * 2 + n].astype(jnp.float32)
                pt[i, n * width : (n + 1) * width, :] = block.T[:width].astype(jnp.bfloat16)
            return 0

        lax.fori_loop(0, rows, transpose, 0)
    for copy in copies[sources:]:
        copy.wait()

    def turn(g, ring):
        nxt = jnp.where(ring == RING - 1, 0, ring + 1)
        start(g + RING, ring)
        wait(nxt)
        for u in range(UNROLL):
            v = list_ref[base + g * UNROLL + u]
            i = v >> 5
            t = i * (nonzeros * per_row * per_row) + (v & 31) * per_row
            result = jnp.dot(pt[i], aps[u][...], preferred_element_type=jnp.float32)
            for n in range(per_row):
                for m in range(per_row):
                    acc = accs[m % naccs]
                    s = tgt_ref[t + n * nonzeros * per_row + m]
                    acc[s] = acc[s] + result[
                        n * width : (n + 1) * width, m * LANES : (m + 1) * LANES
                    ]
            v = list_ref[base + (g + 1) * UNROLL + u]
            j = col_ref[(v >> 5) * nonzeros + (v & 31)]
            right = jnp.concatenate(
                [p_vmem[j >> 1, (j & 1) * 2 + m] for m in range(per_row)], axis=1
            )
            aps[u][...] = jnp.dot(
                a_buf[nxt, u], right, preferred_element_type=jnp.float32
            ).astype(jnp.bfloat16)
        return nxt

    ring = lax.fori_loop(0, turns + 1, turn, jnp.int32(0))
    for _ in range(RING - 1):
        ring = jnp.where(ring == RING - 1, 0, ring + 1)
        wait(ring)

    def total(s):
        value = accs[0][s]
        for acc in accs[1:]:
            value = value + acc[s]
        return value

    if last:
        me = info_ref[cfg["phases"]]

        def emit(q, _):
            for r in range(members):
                s = q * (OWN * members) + (me ^ r) * OWN
                packed = pack_four([total(s + x) for x in range(OWN)], width)
                for t in range(3):
                    out_refs[r][q, t] = packed[t].astype(out_refs[r].dtype)
            return 0

        lax.fori_loop(0, groups, emit, 0)
    else:
        if naccs > 1:

            def fold(s, _):
                accs[0][s] = total(s)
                return 0

            lax.fori_loop(0, slots, fold, 0)
        outs = [pltpu.make_async_copy(accs[0].at[pl.ds(0, slots)], acc_out, sem.at[0])]
        if first:
            outs.append(pltpu.make_async_copy(pt.at[pl.ds(0, rows)], pt_out, sem.at[1]))
        for copy in outs:
            copy.start()
        for copy in outs:
            copy.wait()


def work(cfg, tables, a_rows, packed, pt=None, acc=None):
    width, rows, per_row = cfg["width"], cfg["rows"], cfg["per_row"]
    slots, members, groups = cfg["slots"], cfg["members"], cfg["groups"]
    sources = len(packed)
    cfg = dict(cfg, sources=sources, naccs=2 if slots <= 256 else 1)
    quads = rows * per_row // 4
    hbm = pl.BlockSpec(memory_space=pl.ANY)
    vmem = pl.BlockSpec(memory_space=pltpu.VMEM)
    operands = [a_rows, *packed] + ([] if cfg["first"] else [pt, acc])
    if cfg["last"]:
        shapes = [
            jax.ShapeDtypeStruct((groups, 3, width, LANES), jnp.bfloat16 if r else jnp.float32)
            for r in range(members)
        ]
        out_specs = [vmem] * members
    else:
        shapes = [jax.ShapeDtypeStruct((slots, width, LANES), jnp.float32)]
        if cfg["first"]:
            shapes.append(jax.ShapeDtypeStruct((rows, per_row * width, width), jnp.bfloat16))
        out_specs = [hbm] * len(shapes)
    flops = 2 * rows * cfg["nonzeros"] * 3 * width * width * 2 * width // 3
    return pl.pallas_call(
        functools.partial(work_kernel, cfg),
        grid_spec=pltpu.PrefetchScalarGridSpec(
            num_scalar_prefetch=4,
            grid=(),
            in_specs=[hbm] * len(operands),
            out_specs=out_specs,
            scratch_shapes=[
                pltpu.VMEM((sources * quads, 4, width, LANES), jnp.bfloat16),
                pltpu.VMEM((rows + 1, per_row * width, width), jnp.bfloat16),
                pltpu.VMEM((RING, UNROLL, width, width), jnp.bfloat16),
            ]
            + [pltpu.VMEM((slots + 1, width, LANES), jnp.float32)] * cfg["naccs"]
            + [pltpu.VMEM((width, per_row * LANES), jnp.bfloat16)] * UNROLL
            + [
                pltpu.SemaphoreType.DMA((RING, UNROLL)),
                pltpu.SemaphoreType.DMA((sources + 2,)),
            ],
        ),
        out_shape=shapes,
        compiler_params=pltpu.CompilerParams(vmem_limit_bytes=VMEM_LIMIT),
        cost_estimate=pl.CostEstimate(
            flops=flops, bytes_accessed=20_000_000, transcendentals=0
        ),
        name="work_%d" % cfg["phase"],
    )(*tables, *operands)


def make_tables(columns, targets, me, phase_of, place_of, slots):
    rows, nonzeros = columns.shape
    entries = rows * nonzeros
    phases = max(phase_of) + 1
    list_len = (-(-entries // UNROLL) + RING + 1) * UNROLL
    relative = (columns // rows) ^ me
    phase = sum(jnp.where(relative == r, p, 0) for r, p in enumerate(phase_of))
    place = sum(jnp.where(relative == r, p, 0) for r, p in enumerate(place_of))
    col_table = jnp.pad((place * rows + columns % rows).reshape(-1), (0, nonzeros))
    tgt_table = jnp.pad(
        targets.reshape(-1), (0, targets.shape[1]), constant_values=slots
    )
    flat = phase.reshape(-1)
    order = jnp.arange(entries, dtype=jnp.int32)
    before = (flat[None, :] == flat[:, None]) & (order[None, :] < order[:, None])
    position = flat * list_len + UNROLL + jnp.sum(before.astype(jnp.int32), axis=1)
    counts = jnp.stack([jnp.sum((flat == p).astype(jnp.int32)) for p in range(phases)])
    value = (order // nonzeros) * 32 + order % nonzeros
    dummy = rows * 32
    x = jnp.arange(phases * list_len, dtype=jnp.int32)
    lists = dummy + jnp.sum(
        jnp.where(position[None, :] == x[:, None], value[None, :] - dummy, 0), axis=1
    )
    info = jnp.concatenate([-(-counts // UNROLL), me[None]])
    return (lists.astype(jnp.int32), col_table, tgt_table, info.astype(jnp.int32)), list_len


def shards(a_blocks, col_index, prolong, target):
    rows, nonzeros = a_blocks.shape[1:3]
    per_row = prolong.shape[2]
    width = a_blocks.shape[-1]
    groups = lax.axis_size("grp")
    members = lax.axis_size("blk")
    slots = groups * OWN * members
    me = lax.axis_index("blk").astype(jnp.int32)

    if members == 4:
        phase_of, place_of = [0, 1, 1, 2], [0, 0, 1, 0]
    else:
        phase_of, place_of = [0] + [1] * (members - 1), [0] + list(range(members - 1))
    phases = max(phase_of) + 1

    def exchange(x, r, axis="blk", size=members):
        return lax.ppermute(x, axis, [(d, d ^ r) for d in range(size)])

    own = pack_prolong(prolong)
    packed = [own]
    if members == 4:
        near = [exchange(own, 1), exchange(own, 2)]
        half = own.shape[0] // 2
        far = jnp.concatenate([exchange(near[0][:half], 2), exchange(near[1][half:], 1)])
        packed = [[own], near, [far]]
    else:
        packed = [[own], [exchange(own, r) for r in range(1, members)]]

    tables, list_len = make_tables(col_index[0], target[0], me, phase_of, place_of, slots)
    cfg = dict(
        width=width, rows=rows, nonzeros=nonzeros, per_row=per_row, slots=slots,
        members=members, groups=groups, phases=phases, list_len=list_len,
    )
    a_rows = a_blocks[0]
    pt = acc = None
    for p in range(phases):
        outs = work(
            dict(cfg, phase=p, first=p == 0, last=p == phases - 1),
            tables, a_rows, packed[p], pt, acc,
        )
        if p == 0:
            acc, pt = outs
        elif p < phases - 1:
            (acc,) = outs
    total = outs[0]
    for r in range(1, members):
        total = total + exchange(outs[r], r).astype(jnp.float32)

    rank = lax.axis_index("grp")
    core, chip = rank % 2, rank // 2
    chips = groups // 2
    total = total.reshape(chips, 2, 3, width, LANES)
    give = lax.dynamic_index_in_dim(total, 1 - core, 1, keepdims=False)
    keep = lax.dynamic_index_in_dim(total, core, 1, keepdims=False)
    total = keep + exchange(give, 1, "grp", groups)
    mine = lax.dynamic_index_in_dim(total, chip, 0, keepdims=False)
    for r in range(1, chips):
        part = lax.dynamic_index_in_dim(total, chip ^ r, 0, keepdims=False)
        got = exchange(part.astype(jnp.bfloat16), 2 * r, "grp", groups)
        mine = mine + got.astype(jnp.float32)
    fourth = unpack_last([mine[t] for t in range(3)], width)
    return jnp.concatenate([mine[:, :, :width], fourth[None]])[None]


def solution(mesh):
    return jax.shard_map(
        shards,
        mesh=mesh,
        in_specs=(
            P("grp", "blk", None, None, None),
            P("grp", "blk", None),
            P("grp", "blk", None, None, None),
            P("grp", "blk", None),
        ),
        out_specs=P("grp", "blk", None, None),
        check_vma=False,
    )
```

```python
import functools

import jax
import jax.numpy as jnp
from jax import lax
from jax.experimental import pallas as pl
from jax.experimental.pallas import tpu as pltpu
from jax.sharding import PartitionSpec as P

OWN = 4
UNROLL = 16
LANES = 128
VMEM_LIMIT = 63 * 1024 * 1024
HBM = pl.BlockSpec(memory_space=pl.ANY)


def pack_four(blocks, width):
    strip = LANES - width
    return [
        jnp.concatenate(
            [blocks[t][:, :width], blocks[3][:, strip * t : strip * (t + 1)]], axis=1
        )
        for t in range(3)
    ]


def unpack_last(parts, width):
    return jnp.concatenate([part[:, width:] for part in parts], axis=1)


def pack_kernel(p_ref, out_ref):
    width = p_ref.shape[-1]
    for quad in range(p_ref.shape[0]):
        packed = pack_four([p_ref[quad, t] for t in range(4)], width)
        for t in range(3):
            out_ref[quad, t] = packed[t]


def pack_prolong(prolong):
    width = prolong.shape[-1]
    quads = prolong.shape[1] * prolong.shape[2] // 4
    step = 3
    return pl.pallas_call(
        pack_kernel,
        grid=(quads // step,),
        in_specs=[pl.BlockSpec((step, 4, width, width), lambda g: (g, 0, 0, 0))],
        out_specs=pl.BlockSpec((step, 3, width, LANES), lambda g: (g, 0, 0, 0)),
        out_shape=jax.ShapeDtypeStruct((quads, 3, width, LANES), prolong.dtype),
        name="pack_prolong",
    )(prolong.reshape(quads, 4, width, width))


def work_kernel(cfg, *refs):
    first, last, phase = cfg["first"], cfg["last"], cfg["phase"]
    width, rows, nonzeros, per_row = cfg["width"], cfg["rows"], cfg["nonzeros"], cfg["per_row"]
    slots, members, groups = cfg["slots"], cfg["members"], cfg["groups"]
    refs = list(refs)
    take = lambda n: [refs.pop(0) for _ in range(n)]
    list_ref, info_ref, col_ref, tgt_ref, a_hbm = take(5)
    p_hbm = take(cfg["sources"])
    if not first:
        pt_hbm, acc_in = take(2)
    out_refs = take(2 if first or last else 1)
    p_vmem, pt, a_rows, acc = take(4)
    aps = take(UNROLL)
    a_sem, sem, out_sem = take(3)
    if last:
        stages = take(2)

    base = phase * cfg["list_len"]
    turns = info_ref[phase]
    me, chip, core = [info_ref[cfg["phases"] + x] for x in range(3)]

    def a_copy(i):
        to = a_rows.at[pl.ds(i * nonzeros, nonzeros)]
        return pltpu.make_async_copy(a_hbm.at[i], to, a_sem.at[i])

    def start_row(i, _):
        a_copy(i).start()
        return 0

    def wait_row(i, _):
        a_copy(i).wait()
        return 0

    p_copies, at = [], 0
    for s, source in enumerate(p_hbm):
        to = p_vmem.at[pl.ds(at, source.shape[0]), pl.ds(0, 3)]
        p_copies.append(pltpu.make_async_copy(source, to, sem.at[s]))
        at += source.shape[0]
    others = []
    if not first:
        others.append(pltpu.make_async_copy(pt_hbm, pt, sem.at[cfg["sources"]]))
        others.append(pltpu.make_async_copy(acc_in, acc, sem.at[cfg["sources"] + 1]))
    for copy in p_copies + others:
        copy.start()
    lax.fori_loop(0, rows, start_row, 0)

    a_rows[rows * nonzeros] = jnp.zeros((width, width), a_rows.dtype)
    for ap in aps:
        ap[...] = jnp.zeros_like(ap)
    if first:

        def clear(s, _):
            for x in range(8):
                acc[s * 8 + x] = jnp.zeros((width, LANES), acc.dtype)
            return 0

        lax.fori_loop(0, slots // 8, clear, 0)
    for copy in p_copies:
        copy.wait()

    def unpack(q, _):
        for x in range(2):
            parts = [p_vmem[q * 2 + x, t] for t in range(3)]
            p_vmem[q * 2 + x, 3, :, :width] = unpack_last(parts, width)
        return 0

    lax.fori_loop(0, at // 2, unpack, 0)
    if first:

        def transpose(q, _):
            for x in range(4):
                block = p_vmem[q, x].astype(jnp.float32).T[:width].astype(pt.dtype)
                n = x % per_row
                pt[q * (4 // per_row) + x // per_row, n * width : (n + 1) * width, :] = block
            return 0

        lax.fori_loop(0, at, transpose, 0)
    for copy in others:
        copy.wait()

    scale = 65536 // rows + 1
    assert all((j * scale) >> 16 == j // rows for j in range(rows * members))

    def p_block(i, k):
        j = col_ref[jnp.minimum(i, rows - 1), k]
        member = (j * scale) >> 16
        place = ((member ^ me) - cfg["from"]) * rows + j - member * rows
        return jnp.where(i < rows, place, 0)

    def turn(g, ready):
        need = jnp.minimum((list_ref[base + (g + 2) * UNROLL - 1] >> 5) + 1, rows)
        lax.fori_loop(ready, need, wait_row, 0)

        def products(u):
            v = list_ref[base + g * UNROLL + u]
            i, k = jnp.minimum(v >> 5, rows - 1), v & 31
            partial = jnp.dot(pt[i], aps[u][...], preferred_element_type=jnp.float32)
            w = list_ref[base + (g + 1) * UNROLL + u]
            j = p_block(w >> 5, w & 31)
            right = jnp.concatenate(
                [p_vmem[j >> 1, (j & 1) * 2 + m] for m in range(per_row)], axis=1
            )
            left = a_rows[(w >> 5) * nonzeros + (w & 31)]
            ap = jnp.dot(left, right, preferred_element_type=jnp.float32)
            return u, i, k, partial, ap

        def collect(u, i, k, partial, ap):
            aps[u][...] = ap.astype(jnp.bfloat16)
            for n in range(per_row):
                for m in range(per_row):
                    s = tgt_ref[i, n * nonzeros * per_row + k * per_row + m]
                    acc[s] = acc[s] + partial[
                        n * width : (n + 1) * width, m * LANES : (m + 1) * LANES
                    ]

        held = products(0)
        for u in range(1, UNROLL):
            made = products(u)
            collect(*held)
            held = made
        collect(*held)
        return jnp.maximum(ready, need)

    ready = lax.fori_loop(0, turns + 1, turn, jnp.int32(0))
    lax.fori_loop(ready, rows, wait_row, 0)

    if last:

        def emit(rz, _):
            for rc in range(2):
                for r in range(members):
                    s = ((chip ^ rz) * 2 + (core ^ rc)) * (OWN * members) + (me ^ r) * OWN
                    packed = pack_four([acc[s + x] for x in range(OWN)], width)
                    for t in range(3):
                        stages[rc][rz, r, t] = packed[t].astype(stages[rc].dtype)
                copy = pltpu.make_async_copy(stages[rc].at[rz], out_refs[rc].at[rz], out_sem.at[rc])
                copy.start()
            return 0

        lax.fori_loop(0, groups // 2, emit, 0)
        for rc in range(2):
            pltpu.make_async_copy(stages[rc], out_refs[rc], out_sem.at[rc]).wait()
    else:
        outs = [pltpu.make_async_copy(acc, out_refs[0], out_sem.at[0])]
        if first:
            outs.append(pltpu.make_async_copy(pt, out_refs[1], out_sem.at[1]))
        for copy in outs:
            copy.start()
        for copy in outs:
            copy.wait()


def work(cfg, tables, a_rows, packed, pt=None, acc=None):
    width, rows, nonzeros, per_row = cfg["width"], cfg["rows"], cfg["nonzeros"], cfg["per_row"]
    slots, members, groups = cfg["slots"], cfg["members"], cfg["groups"]
    cfg = dict(cfg, sources=len(packed))
    quads = sum(x.shape[0] for x in packed)
    operands = [a_rows, *packed] + ([] if cfg["first"] else [pt, acc])
    pt_shape = (rows, per_row * width, width)
    stages = []
    if cfg["last"]:
        whole = (groups // 2, members, 3, width, LANES)
        shapes = [jax.ShapeDtypeStruct(whole, jnp.float32), jax.ShapeDtypeStruct(whole, jnp.bfloat16)]
        stages = [pltpu.VMEM(x.shape, x.dtype) for x in shapes]
    else:
        shapes = [jax.ShapeDtypeStruct((slots, width, LANES), jnp.float32)]
        if cfg["first"]:
            shapes.append(jax.ShapeDtypeStruct(pt_shape, jnp.bfloat16))
    return pl.pallas_call(
        functools.partial(work_kernel, cfg),
        grid_spec=pltpu.PrefetchScalarGridSpec(
            num_scalar_prefetch=4,
            grid=(),
            in_specs=[HBM] * len(operands),
            out_specs=[HBM] * len(shapes),
            scratch_shapes=[
                pltpu.VMEM((quads, 4, width, LANES), jnp.bfloat16),
                pltpu.VMEM(pt_shape, jnp.bfloat16),
                pltpu.VMEM((rows * nonzeros + 1, width, width), jnp.bfloat16),
                pltpu.VMEM((slots, width, LANES), jnp.float32),
            ]
            + [pltpu.VMEM((width, per_row * LANES), jnp.bfloat16)] * UNROLL
            + [
                pltpu.SemaphoreType.DMA((rows,)),
                pltpu.SemaphoreType.DMA((len(packed) + 2,)),
                pltpu.SemaphoreType.DMA((2,)),
            ]
            + stages,
        ),
        out_shape=shapes,
        compiler_params=pltpu.CompilerParams(vmem_limit_bytes=VMEM_LIMIT),
        cost_estimate=pl.CostEstimate(
            flops=4 * rows * nonzeros * width * width * width,
            bytes_accessed=20_000_000,
            transcendentals=0,
        ),
        name="work_%d" % cfg["phase"],
    )(*tables, *operands)


def make_lists(columns, place, phase_of):
    rows, nonzeros = columns.shape
    entries = rows * nonzeros
    phases = max(phase_of) + 1
    list_len = (-(-entries // UNROLL) + 2) * UNROLL
    relative = (columns // rows) ^ place[0]
    flat = sum(jnp.where(relative == r, p, 0) for r, p in enumerate(phase_of)).reshape(-1)
    order = jnp.arange(entries, dtype=jnp.int32)
    before = (flat[None, :] == flat[:, None]) & (order[None, :] < order[:, None])
    position = flat * list_len + UNROLL + jnp.sum(before.astype(jnp.int32), axis=1)
    counts = jnp.stack([jnp.sum((flat == p).astype(jnp.int32)) for p in range(phases)])
    value = (order // nonzeros) * 32 + order % nonzeros
    none = rows * 32
    x = jnp.arange(phases * list_len, dtype=jnp.int32)
    lists = none + jnp.sum(
        jnp.where(position[None, :] == x[:, None], value[None, :] - none, 0), axis=1
    )
    info = jnp.concatenate([-(-counts // UNROLL), jnp.stack(place)])
    return lists.astype(jnp.int32), info.astype(jnp.int32), list_len


def shards(a_blocks, col_index, prolong, target):
    rows, nonzeros = a_blocks.shape[1:3]
    per_row = prolong.shape[2]
    width = a_blocks.shape[-1]
    groups = lax.axis_size("grp")
    members = lax.axis_size("blk")
    chips = groups // 2
    slots = groups * OWN * members
    f32, bf16 = jnp.float32, jnp.bfloat16
    rank = lax.axis_index("grp").astype(jnp.int32)
    place = [lax.axis_index("blk").astype(jnp.int32), rank // 2, rank % 2]

    def exchange(x, r, axis="blk", size=members):
        return lax.ppermute(x, axis, [(d, d ^ r) for d in range(size)])

    if members == 4:
        sources = [[0], [1, 2], [3]]
    else:
        sources = [[0]] + [list(range(r, min(r + 3, members))) for r in range(1, members, 3)]
    phases = len(sources)
    phase_of = [p for p in range(phases) for _ in sources[p]]

    own = pack_prolong(prolong)
    near = [exchange(own, r) for r in range(1, 3 if members == 4 else members)]
    lists, info, list_len = make_lists(col_index[0], place, phase_of)
    cfg = dict(
        width=width, rows=rows, nonzeros=nonzeros, per_row=per_row, slots=slots,
        members=members, groups=groups, phases=phases, list_len=list_len,
    )
    packed = [[own]] + [[near[r - 1] for r in s if r <= len(near)] for s in sources[1:]]
    pt = acc = None
    for p in range(phases):
        outs = work(
            {**cfg, "phase": p, "first": p == 0, "last": p == phases - 1, "from": sources[p][0]},
            (lists, info, col_index[0], target[0]), a_blocks[0], packed[p], pt, acc,
        )
        acc = outs[0]
        if p == 0:
            pt = outs[1]
            if members == 4:
                (x, y), _ = lax.optimization_barrier((near, acc))
                half = own.shape[0] // 2
                packed = [[own], [x, y], [exchange(x[:half], 2), exchange(y[half:], 1)]]

    keep, give = outs
    total = keep + exchange(give, 1, "grp", groups).astype(f32)
    half = width // 2
    one, two = total[..., :half, :], total[..., half:, :]
    got = [exchange(one[:, r].astype(bf16), r) for r in range(1, members)]
    sent = [exchange(two[r].astype(bf16), 2 * r, "grp", groups) for r in range(1, chips)]
    got, sent = lax.optimization_barrier((got, sent))
    one, two = one[:, 0], two[0]
    for part in got:
        one = one + part.astype(f32)
    for part in sent:
        two = two + part.astype(f32)
    mine, other = one[0], two[0]
    for r in range(1, chips):
        mine = mine + exchange(one[r].astype(bf16), 2 * r, "grp", groups).astype(f32)
    for r in range(1, members):
        other = other + exchange(two[r].astype(bf16), r).astype(f32)
    mine = jnp.concatenate([mine, other], axis=1)
    fourth = unpack_last([mine[t] for t in range(3)], width)
    return jnp.concatenate([mine[:, :, :width], fourth[None]])[None]


def solution(mesh):
    return jax.shard_map(
        shards,
        mesh=mesh,
        in_specs=(
            P("grp", "blk", None, None, None),
            P("grp", "blk", None),
            P("grp", "blk", None, None, None),
            P("grp", "blk", None),
        ),
        out_specs=P("grp", "blk", None, None),
        check_vma=False,
    )
```

```python
import functools

import jax
import jax.numpy as jnp
from jax import lax
from jax.experimental import pallas as pl
from jax.experimental.pallas import tpu as pltpu
from jax.sharding import PartitionSpec as P

OWN = 4
UNROLL = 16
LANES = 128
AHEAD = 6
VMEM_LIMIT = 63 * 1024 * 1024
HBM = pl.BlockSpec(memory_space=pl.ANY)


def pack_four(blocks, width):
    strip = LANES - width
    return [
        jnp.concatenate(
            [blocks[t][:, :width], blocks[3][:, strip * t : strip * (t + 1)]], axis=1
        )
        for t in range(3)
    ]


def unpack_last(parts, width):
    return jnp.concatenate([part[:, width:] for part in parts], axis=1)


def pack_kernel(p_hbm, *refs):
    outs, (blocks, packed, in_sem, out_sem) = refs[:2], refs[2:]
    width, quads = p_hbm.shape[-1], p_hbm.shape[0]
    steps = in_sem.shape[0]
    size = quads // steps
    half = steps // 2
    loads, stores = [], []
    for c in range(steps):
        part = pl.ds(c * size, size)
        to = outs[c // half].at[pl.ds(c % half * size, size)]
        loads.append(pltpu.make_async_copy(p_hbm.at[part], blocks.at[part], in_sem.at[c]))
        stores.append(pltpu.make_async_copy(packed.at[part], to, out_sem.at[c]))
        loads[c].start()
    for c in range(steps):
        loads[c].wait()
        for quad in range(c * size, (c + 1) * size):
            made = pack_four([blocks[quad, t] for t in range(4)], width)
            for t in range(3):
                packed[quad, t] = made[t]
        stores[c].start()
    for store in stores:
        store.wait()


def pack_prolong(prolong):
    width, dtype = prolong.shape[-1], prolong.dtype
    quads = prolong.shape[1] * prolong.shape[2] // 4
    steps = 4
    return pl.pallas_call(
        pack_kernel,
        in_specs=[HBM],
        out_specs=[HBM] * 2,
        out_shape=[jax.ShapeDtypeStruct((quads // 2, 3, width, LANES), dtype)] * 2,
        scratch_shapes=[
            pltpu.VMEM((quads, 4, width, width), dtype),
            pltpu.VMEM((quads, 3, width, LANES), dtype),
            pltpu.SemaphoreType.DMA((steps,)),
            pltpu.SemaphoreType.DMA((steps,)),
        ],
        compiler_params=pltpu.CompilerParams(vmem_limit_bytes=VMEM_LIMIT),
        name="pack_prolong",
    )(prolong.reshape(quads, 4, width, width))


def work_kernel(cfg, *refs):
    first, last, phase = cfg["first"], cfg["last"], cfg["phase"]
    width, rows, nonzeros, per_row = cfg["width"], cfg["rows"], cfg["nonzeros"], cfg["per_row"]
    slots, members, groups = cfg["slots"], cfg["members"], cfg["groups"]
    refs = list(refs)
    take = lambda n: [refs.pop(0) for _ in range(n)]
    list_ref, col_ref, tgt_ref, a_hbm = take(4)
    p_hbm = take(cfg["sources"])
    if not first:
        (pt_hbm,) = take(1)
    acc_in = take(cfg["sums"])
    out_refs = take(2 if first or last else 1)
    p_vmem, pt, a_rows, acc = take(4)
    aps = take(UNROLL)
    a_sem, sem, out_sem = take(3)
    stages = take(2 if last else 0)
    late = take(len(acc_in) if cfg["late"] else 0)

    me = lax.axis_index("blk").astype(jnp.int32)
    rank = lax.axis_index("grp").astype(jnp.int32)
    chip, core = rank >> 1, rank & 1

    def a_copy(i):
        to = a_rows.at[pl.ds(i * nonzeros, nonzeros)]
        return pltpu.make_async_copy(a_hbm.at[i], to, a_sem.at[i])

    def start_row(i, _):
        a_copy(i).start()
        return 0

    def wait_row(i, _):
        a_copy(i).wait()

        @pl.when(i + AHEAD < rows)
        def _():
            a_copy(i + AHEAD).start()

        return 0

    p_copies, at = [], 0
    for s, source in enumerate(p_hbm):
        to = p_vmem.at[pl.ds(at, source.shape[0]), pl.ds(0, 3)]
        p_copies.append(pltpu.make_async_copy(source, to, sem.at[s]))
        at += source.shape[0]
    others = []
    if not first:
        others.append(pltpu.make_async_copy(pt_hbm, pt, sem.at[cfg["sources"]]))
    sums = [
        pltpu.make_async_copy(source, to, sem.at[cfg["sources"] + 1 + s])
        for s, (source, to) in enumerate(zip(acc_in, late or [acc]))
    ]
    for copy in p_copies + others + ([] if late else sums):
        copy.start()
    lax.fori_loop(0, AHEAD, start_row, 0)

    a_rows[rows * nonzeros] = jnp.zeros((width, width), a_rows.dtype)
    if late or not acc_in:

        def clear(s, _):
            for x in range(8):
                acc[s * 8 + x] = jnp.zeros((width, LANES), acc.dtype)
            return 0

        lax.fori_loop(0, slots // 8, clear, 0)
    for copy in p_copies:
        copy.wait()

    def unpack(q, _):
        for x in range(2):
            parts = [p_vmem[q * 2 + x, t] for t in range(3)]
            p_vmem[q * 2 + x, 3, :, :width] = unpack_last(parts, width)
        return 0

    lax.fori_loop(0, at // 2, unpack, 0)
    if first:

        def transpose(q, _):
            for x in range(4):
                block = p_vmem[q, x].T[:width]
                n = x % per_row
                pt[q * (4 // per_row) + x // per_row, n * width : (n + 1) * width, :] = block
            return 0

        lax.fori_loop(0, at, transpose, 0)
    for copy in others + ([] if late else sums):
        copy.wait()
    if late:
        for copy in sums:
            copy.start()

    scale = 65536 // rows + 1
    assert all((j * scale) >> 16 == j // rows for j in range(rows * members))

    def p_block(i, k):
        j = col_ref[jnp.minimum(i, rows - 1), k]
        member = (j * scale) >> 16
        place = ((member ^ me) - cfg["from"]) * rows + j - member * rows
        return jnp.where(i < rows, place, 0)

    def first_product(g, u):
        w = list_ref[phase, g * UNROLL + u]
        j = p_block(w >> 5, w & 31)
        right = jnp.concatenate(
            [p_vmem[j >> 1, (j & 1) * 2 + m] for m in range(per_row)], axis=1
        )
        left = a_rows[(w >> 5) * nonzeros + (w & 31)]
        return jnp.dot(left, right, preferred_element_type=jnp.float32)

    def second_product(u, i):
        return jnp.dot(pt[i], aps[u][...], preferred_element_type=jnp.float32)

    def entry(g, u):
        v = list_ref[phase, g * UNROLL + u]
        return jnp.minimum(v >> 5, rows - 1), v & 31

    def keep(u, ap):
        aps[u][...] = ap.astype(jnp.bfloat16)

    def collect(i, k, partial):
        for n in range(per_row):
            for m in range(per_row):
                s = tgt_ref[i, n * nonzeros * per_row + k * per_row + m]
                acc[s] = acc[s] + partial[
                    n * width : (n + 1) * width, m * LANES : (m + 1) * LANES
                ]

    def rows_for(g, ready):
        need = jnp.minimum((list_ref[phase, (g + 1) * UNROLL - 1] >> 5) + 1, rows)
        lax.fori_loop(ready, need, wait_row, 0)
        return jnp.maximum(ready, need)

    def turn(carry):
        g, ready = carry
        ready = rows_for(g + 1, ready)
        held = None
        for u in range(UNROLL):
            i, k = entry(g, u)
            made = u, i, k, second_product(u, i), first_product(g + 1, u)
            if held is not None:
                keep(held[0], held[4])
                collect(*held[1:4])
            held = made
        keep(held[0], held[4])
        collect(*held[1:4])
        return g + 1, ready

    ready = rows_for(0, jnp.int32(0))
    for u in range(UNROLL):
        keep(u, first_product(0, u))
    g, ready = lax.while_loop(
        lambda c: list_ref[phase, (c[0] + 1) * UNROLL] < rows * 32, turn, (jnp.int32(0), ready)
    )
    for u in range(UNROLL):
        i, k = entry(g, u)
        collect(i, k, second_product(u, i))
    lax.fori_loop(ready, rows, wait_row, 0)
    if late:
        for copy in sums:
            copy.wait()

    def total(s):
        value = acc[s]
        for extra in late:
            value = value + extra[s]
        return value

    if last:

        def emit(rz, _):
            for rc in range(2):
                for r in range(members):
                    s = ((chip ^ rz) * 2 + (core ^ rc)) * (OWN * members) + (me ^ r) * OWN
                    packed = pack_four([total(s + x) for x in range(OWN)], width)
                    for t in range(3):
                        stages[rc][rz, r, t] = packed[t].astype(stages[rc].dtype)
                copy = pltpu.make_async_copy(stages[rc].at[rz], out_refs[rc].at[rz], out_sem.at[rc])
                copy.start()
            return 0

        lax.fori_loop(0, groups // 2, emit, 0)
        for rc in range(2):
            pltpu.make_async_copy(stages[rc], out_refs[rc], out_sem.at[rc]).wait()
    else:
        outs = [pltpu.make_async_copy(acc, out_refs[0], out_sem.at[0])]
        if first:
            outs.append(pltpu.make_async_copy(pt, out_refs[1], out_sem.at[1]))
        for copy in outs:
            copy.start()
        for copy in outs:
            copy.wait()


def work(cfg, tables, a_rows, packed, pt=None, sums=()):
    width, rows, nonzeros, per_row = cfg["width"], cfg["rows"], cfg["nonzeros"], cfg["per_row"]
    slots, members, groups = cfg["slots"], cfg["members"], cfg["groups"]
    late = cfg["last"] and cfg["late"]
    cfg = dict(cfg, sources=len(packed), sums=len(sums), late=late)
    quads = sum(x.shape[0] for x in packed)
    operands = [a_rows, *packed] + ([] if cfg["first"] else [pt]) + list(sums)
    pt_shape = (rows, per_row * width, width)
    stages = []
    if cfg["last"]:
        whole = (groups // 2, members, 3, width, LANES)
        shapes = [jax.ShapeDtypeStruct(whole, jnp.float32), jax.ShapeDtypeStruct(whole, jnp.bfloat16)]
        stages = [pltpu.VMEM(x.shape, x.dtype) for x in shapes]
    else:
        shapes = [jax.ShapeDtypeStruct((slots, width, LANES), jnp.float32)]
        if cfg["first"]:
            shapes.append(jax.ShapeDtypeStruct(pt_shape, jnp.bfloat16))
    return pl.pallas_call(
        functools.partial(work_kernel, cfg),
        grid_spec=pltpu.PrefetchScalarGridSpec(
            num_scalar_prefetch=3,
            grid=(),
            in_specs=[HBM] * len(operands),
            out_specs=[HBM] * len(shapes),
            scratch_shapes=[
                pltpu.VMEM((quads, 4, width, LANES), jnp.bfloat16),
                pltpu.VMEM(pt_shape, jnp.bfloat16),
                pltpu.VMEM((rows * nonzeros + 1, width, width), jnp.bfloat16),
                pltpu.VMEM((slots, width, LANES), jnp.float32),
            ]
            + [pltpu.VMEM((width, per_row * LANES), jnp.bfloat16)] * UNROLL
            + [
                pltpu.SemaphoreType.DMA((rows,)),
                pltpu.SemaphoreType.DMA((len(packed) + 1 + len(sums),)),
                pltpu.SemaphoreType.DMA((2,)),
            ]
            + stages
            + [pltpu.VMEM((slots, width, LANES), jnp.float32)] * (len(sums) if late else 0),
        ),
        out_shape=shapes,
        compiler_params=pltpu.CompilerParams(vmem_limit_bytes=VMEM_LIMIT),
        cost_estimate=pl.CostEstimate(
            flops=4 * rows * nonzeros * width * width * width,
            bytes_accessed=20_000_000,
            transcendentals=0,
        ),
        name="work_%d" % cfg["phase"],
    )(*tables, *operands)


def make_lists(columns, me, phase_of):
    rows, nonzeros = columns.shape
    entries = rows * nonzeros
    phases = max(phase_of) + 1
    list_len = (-(-entries // UNROLL) + 1) * UNROLL
    relative = (columns.reshape(-1) // rows) ^ me
    flat = sum(jnp.where(relative == r, p, 0) for r, p in enumerate(phase_of))
    order = jnp.arange(entries, dtype=jnp.int32)
    before = (flat[None, :] == flat[:, None]) & (order[None, :] < order[:, None])
    position = flat * list_len + jnp.sum(before.astype(jnp.int32), axis=1)
    value = (order // nonzeros) * 32 + order % nonzeros
    none = rows * 32
    x = jnp.arange(phases * list_len, dtype=jnp.int32).reshape(phases, list_len)
    found = jnp.where(position[:, None, None] == x[None], (value - none)[:, None, None], 0)
    return none + jnp.sum(found, axis=0)


def shards(a_blocks, col_index, prolong, target):
    rows, nonzeros = a_blocks.shape[1:3]
    per_row = prolong.shape[2]
    width = a_blocks.shape[-1]
    groups = lax.axis_size("grp")
    members = lax.axis_size("blk")
    chips = groups // 2
    slots = groups * OWN * members
    f32, bf16 = jnp.float32, jnp.bfloat16
    me = lax.axis_index("blk").astype(jnp.int32)

    def exchange(x, r, axis="blk", size=members):
        return lax.ppermute(x, axis, [(d, d ^ r) for d in range(size)])

    if members == 4:
        sources = [[0], [1, 2], [3]]
    else:
        sources = [[0]] + [list(range(r, min(r + 3, members))) for r in range(1, members, 3)]
    phases = len(sources)
    phase_of = [p for p in range(phases) for _ in sources[p]]

    own = pack_prolong(prolong)
    direct = range(1, 3 if members == 4 else members)
    packed = {0: own, **{r: [exchange(x, r) for x in own] for r in direct}}
    lists = make_lists(col_index[0], me, phase_of)
    cfg = dict(
        width=width, rows=rows, nonzeros=nonzeros, per_row=per_row, slots=slots,
        members=members, groups=groups, late=slots <= 128,
    )
    pt, sums = None, []
    for p in range(phases):
        last = p == phases - 1
        use = [x for r in sources[p] for x in packed[r]]
        before = (sums if last else []) if cfg["late"] else sums[-1:]
        outs = work(
            {**cfg, "phase": p, "first": p == 0, "last": last, "from": sources[p][0]},
            (lists, col_index[0], target[0]), a_blocks[0], use, pt, before,
        )
        sums = sums + [outs[0]]
        if p == 0:
            pt = outs[1]
            if members == 4:
                near, _ = lax.optimization_barrier((packed[1] + packed[2], outs[0]))
                packed = {0: own, 1: near[:2], 2: near[2:]}
                packed[3] = [exchange(near[0], 2), exchange(near[3], 1)]

    keep, give = outs
    total = keep + exchange(give, 1, "grp", groups).astype(f32)
    half = width // 3 * 2
    one, two = total[..., :half, :], total[..., half:, :]
    got = [exchange(one[:, r].astype(bf16), r) for r in range(1, members)]
    sent = [exchange(two[r].astype(bf16), 2 * r, "grp", groups) for r in range(1, chips)]
    got, sent = lax.optimization_barrier((got, sent))
    one, two = one[:, 0], two[0]
    for part in got:
        one = one + part.astype(f32)
    for part in sent:
        two = two + part.astype(f32)
    mine, other = one[0], two[0]
    for r in range(1, chips):
        mine = mine + exchange(one[r].astype(bf16), 2 * r, "grp", groups).astype(f32)
    for r in range(1, members):
        other = other + exchange(two[r].astype(bf16), r).astype(f32)
    mine = jnp.concatenate([mine, other], axis=1)
    fourth = unpack_last([mine[t] for t in range(3)], width)
    return jnp.concatenate([mine[:, :, :width], fourth[None]])[None]


def solution(mesh):
    return jax.shard_map(
        shards,
        mesh=mesh,
        in_specs=(
            P("grp", "blk", None, None, None),
            P("grp", "blk", None),
            P("grp", "blk", None, None, None),
            P("grp", "blk", None),
        ),
        out_specs=P("grp", "blk", None, None),
        check_vma=False,
    )
```

```python
import functools

import jax
import jax.numpy as jnp
from jax import lax
from jax.experimental import pallas as pl
from jax.experimental.pallas import tpu as pltpu
from jax.sharding import PartitionSpec as P

OWN = 4
UNROLL = 16
LANES = 128
AHEAD = 12
VMEM_LIMIT = 63 * 1024 * 1024
HBM = pl.BlockSpec(memory_space=pl.ANY)


def pack_four(blocks, width):
    strip = LANES - width
    return [
        jnp.concatenate(
            [blocks[t][:, :width], blocks[3][:, strip * t : strip * (t + 1)]], axis=1
        )
        for t in range(3)
    ]


def unpack_last(parts, width):
    return jnp.concatenate([part[:, width:] for part in parts], axis=1)


def pack_kernel(p_hbm, *refs):
    out, blocks, packed, in_sem, out_sem = refs
    width, quads = p_hbm.shape[-1], p_hbm.shape[0]
    steps = in_sem.shape[0]
    size = quads // steps
    loads, stores = [], []
    for c in range(steps):
        part = pl.ds(c * size, size)
        loads.append(pltpu.make_async_copy(p_hbm.at[part], blocks.at[part], in_sem.at[c]))
        stores.append(pltpu.make_async_copy(packed.at[part], out.at[part], out_sem.at[c]))
        loads[c].start()
    for c in range(steps):
        loads[c].wait()
        for quad in range(c * size, (c + 1) * size):
            made = pack_four([blocks[quad, t] for t in range(4)], width)
            for t in range(3):
                packed[quad, t] = made[t]
        stores[c].start()
    for store in stores:
        store.wait()


def pack_prolong(prolong):
    width, dtype = prolong.shape[-1], prolong.dtype
    quads = prolong.shape[1] * prolong.shape[2] // 4
    steps = 4
    return pl.pallas_call(
        pack_kernel,
        in_specs=[HBM],
        out_specs=HBM,
        out_shape=jax.ShapeDtypeStruct((quads, 3, width, LANES), dtype),
        scratch_shapes=[
            pltpu.VMEM((quads, 4, width, width), dtype),
            pltpu.VMEM((quads, 3, width, LANES), dtype),
            pltpu.SemaphoreType.DMA((steps,)),
            pltpu.SemaphoreType.DMA((steps,)),
        ],
        compiler_params=pltpu.CompilerParams(vmem_limit_bytes=VMEM_LIMIT),
        name="pack_prolong",
    )(prolong.reshape(quads, 4, width, width))


def divider(rows, members):
    scale = 65536 // rows + 1
    assert all((x * scale) >> 16 == x // rows for x in range(rows * members))
    return scale


def work_kernel(cfg, *refs):
    first, last, phase = cfg["first"], cfg["last"], cfg["phase"]
    width, rows, nonzeros, per_row = cfg["width"], cfg["rows"], cfg["nonzeros"], cfg["per_row"]
    slots, members, groups = cfg["slots"], cfg["members"], cfg["groups"]
    refs = list(refs)
    take = lambda n: [refs.pop(0) for _ in range(n)]
    list_ref, col_ref, tgt_ref, a_hbm = take(4)
    p_hbm = take(cfg["sources"])
    if not first:
        (pt_hbm,) = take(1)
    acc_in = take(cfg["sums"])
    out_refs = take(2 if first or last else 1)
    p_vmem, pt, a_rows, acc = take(4)
    aps = take(UNROLL)
    a_sem, sem, out_sem = take(3)
    stages = take(2 if last else 0)
    late = take(len(acc_in) if cfg["late"] else 0)

    me = lax.axis_index("blk").astype(jnp.int32)
    rank = lax.axis_index("grp").astype(jnp.int32)
    chip, core = rank >> 1, rank & 1

    def a_copy(i):
        to = a_rows.at[pl.ds((i + 1) * nonzeros, nonzeros)]
        return pltpu.make_async_copy(a_hbm.at[i], to, a_sem.at[i])

    def start_row(i, _):
        a_copy(i).start()
        return 0

    def wait_row(i, _):
        a_copy(i).wait()

        @pl.when(i + AHEAD < rows)
        def _():
            a_copy(i + AHEAD).start()

        if late:

            @pl.when(i + AHEAD == rows - 1)
            def _():
                for copy in sums:
                    copy.start()

        return 0

    p_copies, at = [], 0
    for s, source in enumerate(p_hbm):
        to = p_vmem.at[pl.ds(at, source.shape[0]), pl.ds(0, 3)]
        p_copies.append(pltpu.make_async_copy(source, to, sem.at[s]))
        at += source.shape[0]
    others = []
    if not first:
        others.append(pltpu.make_async_copy(pt_hbm, pt, sem.at[cfg["sources"]]))
    sums = [
        pltpu.make_async_copy(source, to, sem.at[cfg["sources"] + 1 + s])
        for s, (source, to) in enumerate(zip(acc_in, late or [acc]))
    ]
    for copy in p_copies + others + ([] if late else sums):
        copy.start()
    lax.fori_loop(0, AHEAD, start_row, 0)

    a_rows[0] = jnp.zeros((width, width), a_rows.dtype)
    if late or not acc_in:

        def clear(s, _):
            for x in range(8):
                acc[s * 8 + x] = jnp.zeros((width, LANES), acc.dtype)
            return 0

        lax.fori_loop(0, slots // 8, clear, 0)
    for copy in p_copies:
        copy.wait()

    def unpack(q, _):
        for x in range(2):
            parts = [p_vmem[q * 2 + x, t] for t in range(3)]
            p_vmem[q * 2 + x, 3, :, :width] = unpack_last(parts, width)
        return 0

    lax.fori_loop(0, at // 2, unpack, 0)
    if first:

        def transpose(q, _):
            for x in range(4):
                block = p_vmem[q, x].T[:width]
                n = x % per_row
                pt[q * (4 // per_row) + x // per_row, n * width : (n + 1) * width, :] = block
            return 0

        lax.fori_loop(0, at, transpose, 0)
    for copy in others + ([] if late else sums):
        copy.wait()

    scale = divider(rows, members)

    def p_block(v):
        j = col_ref[jnp.maximum((v >> 5) - 1, 0), v & 31]
        member = (j * scale) >> 16
        place = ((member ^ me) - cfg["from"]) * rows + j - member * rows
        return jnp.where(v > 0, place, 0)

    def first_product(g, u):
        w = list_ref[phase, g * UNROLL + u]
        j = p_block(w)
        right = jnp.concatenate(
            [p_vmem[j >> 1, (j & 1) * 2 + m] for m in range(per_row)], axis=1
        )
        left = a_rows[(w >> 5) * nonzeros + (w & 31)]
        return jnp.dot(left, right, preferred_element_type=jnp.float32)

    def second_product(u, i):
        return jnp.dot(pt[i], aps[u][...], preferred_element_type=jnp.float32)

    def entry(g, u):
        v = list_ref[phase, g * UNROLL + u]
        return jnp.maximum((v >> 5) - 1, 0), v & 31

    def keep(u, ap):
        aps[u][...] = ap.astype(jnp.bfloat16)

    def collect(i, k, partial):
        for n in range(per_row):
            for m in range(per_row):
                s = tgt_ref[i, n * nonzeros * per_row + k * per_row + m]
                acc[s] = acc[s] + partial[
                    n * width : (n + 1) * width, m * LANES : (m + 1) * LANES
                ]

    def rows_for(g, ready):
        v = list_ref[phase, (g + 1) * UNROLL - 1]
        need = jnp.where(v > 0, v >> 5, rows)
        lax.fori_loop(ready, need, wait_row, 0)
        return jnp.maximum(ready, need)

    def turn(carry):
        g, ready = carry
        ready = rows_for(g + 1, ready)
        held = None
        for u in range(UNROLL):
            i, k = entry(g, u)
            made = u, i, k, second_product(u, i), first_product(g + 1, u)
            if held is not None:
                keep(held[0], held[4])
                collect(*held[1:4])
            held = made
        keep(held[0], held[4])
        collect(*held[1:4])
        return g + 1, ready

    ready = rows_for(0, jnp.int32(0))
    for u in range(UNROLL):
        keep(u, first_product(0, u))
    g, ready = lax.while_loop(
        lambda c: list_ref[phase, (c[0] + 1) * UNROLL] > 0, turn, (jnp.int32(0), ready)
    )
    for u in range(UNROLL):
        i, k = entry(g, u)
        collect(i, k, second_product(u, i))
    lax.fori_loop(ready, rows, wait_row, 0)
    if late:
        for copy in sums:
            copy.wait()

    def total(s):
        value = acc[s]
        for extra in late:
            value = value + extra[s]
        return value

    if last:

        def emit(rz, _):
            for rc in range(2):
                for r in range(members):
                    s = ((chip ^ rz) * 2 + (core ^ rc)) * (OWN * members) + (me ^ r) * OWN
                    packed = pack_four([total(s + x) for x in range(OWN)], width)
                    for t in range(3):
                        stages[rc][rz, r, t] = packed[t].astype(stages[rc].dtype)
                copy = pltpu.make_async_copy(stages[rc].at[rz], out_refs[rc].at[rz], out_sem.at[rc])
                copy.start()
            return 0

        lax.fori_loop(0, groups // 2, emit, 0)
        for rc in range(2):
            pltpu.make_async_copy(stages[rc], out_refs[rc], out_sem.at[rc]).wait()
    else:
        outs = [pltpu.make_async_copy(acc, out_refs[0], out_sem.at[0])]
        if first:
            outs.append(pltpu.make_async_copy(pt, out_refs[1], out_sem.at[1]))
        for copy in outs:
            copy.start()
        for copy in outs:
            copy.wait()


def work(cfg, tables, a_rows, packed, pt=None, sums=()):
    width, rows, nonzeros, per_row = cfg["width"], cfg["rows"], cfg["nonzeros"], cfg["per_row"]
    slots, members, groups = cfg["slots"], cfg["members"], cfg["groups"]
    late = cfg["last"] and cfg["late"]
    cfg = dict(cfg, sources=len(packed), sums=len(sums), late=late)
    quads = sum(x.shape[0] for x in packed)
    operands = [a_rows, *packed] + ([] if cfg["first"] else [pt]) + list(sums)
    pt_shape = (rows, per_row * width, width)
    stages = []
    if cfg["last"]:
        whole = (groups // 2, members, 3, width, LANES)
        shapes = [jax.ShapeDtypeStruct(whole, jnp.float32), jax.ShapeDtypeStruct(whole, jnp.bfloat16)]
        stages = [pltpu.VMEM(x.shape, x.dtype) for x in shapes]
    else:
        shapes = [jax.ShapeDtypeStruct((slots, width, LANES), jnp.float32)]
        if cfg["first"]:
            shapes.append(jax.ShapeDtypeStruct(pt_shape, jnp.bfloat16))
    return pl.pallas_call(
        functools.partial(work_kernel, cfg),
        grid_spec=pltpu.PrefetchScalarGridSpec(
            num_scalar_prefetch=3,
            grid=(),
            in_specs=[HBM] * len(operands),
            out_specs=[HBM] * len(shapes),
            scratch_shapes=[
                pltpu.VMEM((quads, 4, width, LANES), jnp.bfloat16),
                pltpu.VMEM(pt_shape, jnp.bfloat16),
                pltpu.VMEM(((rows + 1) * nonzeros, width, width), jnp.bfloat16),
                pltpu.VMEM((slots, width, LANES), jnp.float32),
            ]
            + [pltpu.VMEM((width, per_row * LANES), jnp.bfloat16)] * UNROLL
            + [
                pltpu.SemaphoreType.DMA((rows,)),
                pltpu.SemaphoreType.DMA((len(packed) + 1 + len(sums),)),
                pltpu.SemaphoreType.DMA((2,)),
            ]
            + stages
            + [pltpu.VMEM((slots, width, LANES), jnp.float32)] * (len(sums) if late else 0),
        ),
        out_shape=shapes,
        compiler_params=pltpu.CompilerParams(vmem_limit_bytes=VMEM_LIMIT),
        cost_estimate=pl.CostEstimate(
            flops=4 * rows * nonzeros * width * width * width,
            bytes_accessed=20_000_000,
            transcendentals=0,
        ),
        name="work_%d" % cfg["phase"],
    )(*tables, *operands)


def make_lists(columns, me, phase_of):
    rows, nonzeros = columns.shape
    entries = rows * nonzeros
    phases = max(phase_of) + 1
    list_len = (-(-entries // UNROLL) + 1) * UNROLL
    relative = ((columns * divider(rows, lax.axis_size("blk"))) >> 16) ^ me
    flat = sum(jnp.where(relative == r, p, 0) for r, p in enumerate(phase_of)).reshape(-1)
    order = jnp.arange(entries, dtype=jnp.int32)
    before = (flat[None, :] == flat[:, None]) & (order[None, :] < order[:, None])
    position = flat * list_len + jnp.sum(before.astype(jnp.int32), axis=1)
    value = (order // nonzeros + 1) * 32 + order % nonzeros
    x = jnp.arange(phases * list_len, dtype=jnp.int32).reshape(phases, list_len)
    found = jnp.where(position[:, None, None] == x[None], value[:, None, None], 0)
    return jnp.sum(found, axis=0)


def shards(a_blocks, col_index, prolong, target):
    rows, nonzeros = a_blocks.shape[1:3]
    per_row = prolong.shape[2]
    width = a_blocks.shape[-1]
    groups = lax.axis_size("grp")
    members = lax.axis_size("blk")
    chips = groups // 2
    slots = groups * OWN * members
    f32, bf16 = jnp.float32, jnp.bfloat16
    me = lax.axis_index("blk").astype(jnp.int32)

    def exchange(x, r, axis="blk", size=members):
        return lax.ppermute(x, axis, [(d, d ^ r) for d in range(size)])

    if members == 4:
        sources = [[0], [1, 2], [3]]
    else:
        sources = [[0]] + [list(range(r, min(r + 3, members))) for r in range(1, members, 3)]
    phases = len(sources)
    phase_of = [p for p in range(phases) for _ in sources[p]]

    own = pack_prolong(prolong)
    packed = [own] + [exchange(own, r) for r in range(1, members)]
    lists = make_lists(col_index[0], me, phase_of)
    cfg = dict(
        width=width, rows=rows, nonzeros=nonzeros, per_row=per_row, slots=slots,
        members=members, groups=groups, late=slots <= 128,
    )
    pt, sums = None, []
    for p in range(phases):
        last = p == phases - 1
        use = [packed[r] for r in sources[p]]
        before = (sums if last else []) if cfg["late"] else sums[-1:]
        outs = work(
            {**cfg, "phase": p, "first": p == 0, "last": last, "from": sources[p][0]},
            (lists, col_index[0], target[0]), a_blocks[0], use, pt, before,
        )
        sums = sums + [outs[0]]
        if p == 0:
            pt = outs[1]

    keep, give = outs
    total = keep + exchange(give, 1, "grp", groups).astype(f32)
    got = [exchange(total[:, r].astype(bf16), r) for r in range(1, members)]
    total = total[:, 0]
    for part in got:
        total = total + part.astype(f32)
    got = [exchange(total[r].astype(bf16), 2 * r, "grp", groups) for r in range(1, chips)]
    mine = total[0]
    for part in got:
        mine = mine + part.astype(f32)
    fourth = unpack_last([mine[t] for t in range(3)], width)
    return jnp.concatenate([mine[:, :, :width], fourth[None]])[None]


def solution(mesh):
    return jax.shard_map(
        shards,
        mesh=mesh,
        in_specs=(
            P("grp", "blk", None, None, None),
            P("grp", "blk", None),
            P("grp", "blk", None, None, None),
            P("grp", "blk", None),
        ),
        out_specs=P("grp", "blk", None, None),
        check_vma=False,
    )
```

```python
import functools

import jax
import jax.numpy as jnp
from jax import lax
from jax.experimental import pallas as pl
from jax.experimental.pallas import tpu as pltpu
from jax.sharding import PartitionSpec as P

OWN = 4
UNROLL = 16
LANES = 128
AHEAD = 12
VMEM_LIMIT = 65408 * 1024
HBM = pl.BlockSpec(memory_space=pl.ANY)


def pack_four(blocks, width):
    strip = LANES - width
    return [
        jnp.concatenate(
            [blocks[t][:, :width], blocks[3][:, strip * t : strip * (t + 1)]], axis=1
        )
        for t in range(3)
    ]


def unpack_last(parts, width):
    return jnp.concatenate([part[:, width:] for part in parts], axis=1)


def pack_kernel(p_hbm, *refs):
    out, blocks, packed, in_sem, out_sem = refs
    width, quads = p_hbm.shape[-1], p_hbm.shape[0]
    steps = in_sem.shape[0]
    size = quads // steps
    loads, stores = [], []
    for c in range(steps):
        part = pl.ds(c * size, size)
        loads.append(pltpu.make_async_copy(p_hbm.at[part], blocks.at[part], in_sem.at[c]))
        stores.append(pltpu.make_async_copy(packed.at[part], out.at[part], out_sem.at[c]))
        loads[c].start()
    for c in range(steps):
        loads[c].wait()
        for quad in range(c * size, (c + 1) * size):
            made = pack_four([blocks[quad, t] for t in range(4)], width)
            for t in range(3):
                packed[quad, t] = made[t]
        stores[c].start()
    for store in stores:
        store.wait()


def pack_prolong(prolong):
    width, dtype = prolong.shape[-1], prolong.dtype
    quads = prolong.shape[1] * prolong.shape[2] // 4
    steps = 4
    return pl.pallas_call(
        pack_kernel,
        in_specs=[HBM],
        out_specs=HBM,
        out_shape=jax.ShapeDtypeStruct((quads, 3, width, LANES), dtype),
        scratch_shapes=[
            pltpu.VMEM((quads, 4, width, width), dtype),
            pltpu.VMEM((quads, 3, width, LANES), dtype),
            pltpu.SemaphoreType.DMA((steps,)),
            pltpu.SemaphoreType.DMA((steps,)),
        ],
        compiler_params=pltpu.CompilerParams(vmem_limit_bytes=VMEM_LIMIT),
        name="pack_prolong",
    )(prolong.reshape(quads, 4, width, width))


def divider(rows, members):
    scale = 65536 // rows + 1
    assert all((x * scale) >> 16 == x // rows for x in range(rows * members))
    return scale


def work_kernel(cfg, *refs):
    first, last, phase = cfg["first"], cfg["last"], cfg["phase"]
    width, rows, nonzeros, per_row = cfg["width"], cfg["rows"], cfg["nonzeros"], cfg["per_row"]
    slots, members, groups = cfg["slots"], cfg["members"], cfg["groups"]
    refs = list(refs)
    take = lambda n: [refs.pop(0) for _ in range(n)]
    list_ref, col_ref, tgt_ref, a_hbm = take(4)
    p_hbm = take(cfg["sources"])
    if not first:
        (pt_hbm,) = take(1)
    acc_in = take(cfg["sums"])
    out_refs = take(2 if first or last else 1)
    p_vmem, pt, a_rows, acc = take(4)
    aps = take(UNROLL)
    a_sem, sem, out_sem = take(3)
    stages = take(2 if last else 0)
    late = take(len(acc_in) if cfg["late"] else 0)

    me = lax.axis_index("blk").astype(jnp.int32)
    rank = lax.axis_index("grp").astype(jnp.int32)
    core = rank & 1

    def a_copy(i):
        to = a_rows.at[pl.ds((i + 1) * nonzeros, nonzeros)]
        return pltpu.make_async_copy(a_hbm.at[i], to, a_sem.at[i])

    def start_row(i, _):
        a_copy(i).start()
        return 0

    def wait_row(i, _):
        a_copy(i).wait()

        @pl.when(i + AHEAD < rows)
        def _():
            a_copy(i + AHEAD).start()

        if late:

            @pl.when(i + AHEAD == rows - 1)
            def _():
                for copy in sums:
                    copy.start()

        return 0

    p_copies, at = [], 0
    for s, source in enumerate(p_hbm):
        to = p_vmem.at[pl.ds(at, source.shape[0]), pl.ds(0, 3)]
        p_copies.append(pltpu.make_async_copy(source, to, sem.at[s]))
        at += source.shape[0]
    others = []
    if not first:
        others.append(pltpu.make_async_copy(pt_hbm, pt, sem.at[cfg["sources"]]))
    sums = [
        pltpu.make_async_copy(source, to, sem.at[cfg["sources"] + 1 + s])
        for s, (source, to) in enumerate(zip(acc_in, late or [acc]))
    ]
    for copy in p_copies + others + ([] if late else sums):
        copy.start()
    lax.fori_loop(0, AHEAD, start_row, 0)

    a_rows[0] = jnp.zeros((width, width), a_rows.dtype)
    if late or not acc_in:

        def clear(s, _):
            for x in range(8):
                acc[s * 8 + x] = jnp.zeros((width, LANES), acc.dtype)
            return 0

        lax.fori_loop(0, slots // 8, clear, 0)
    for copy in p_copies:
        copy.wait()

    def unpack(q, _):
        for x in range(2):
            parts = [p_vmem[q * 2 + x, t] for t in range(3)]
            p_vmem[q * 2 + x, 3, :, :width] = unpack_last(parts, width)
        return 0

    lax.fori_loop(0, at // 2, unpack, 0)
    if first:

        def transpose(q, _):
            for x in range(4):
                block = p_vmem[q, x].T[:width]
                n = x % per_row
                pt[q * (4 // per_row) + x // per_row, n * width : (n + 1) * width, :] = block
            return 0

        lax.fori_loop(0, at, transpose, 0)
    for copy in others + ([] if late else sums):
        copy.wait()

    scale = divider(rows, members)

    def p_block(v):
        j = col_ref[jnp.maximum((v >> 5) - 1, 0), v & 31]
        member = (j * scale) >> 16
        place = ((member ^ me) - cfg["from"]) * rows + j - member * rows
        return jnp.where(v > 0, place, 0)

    def first_product(g, u):
        w = list_ref[phase, g * UNROLL + u]
        j = p_block(w)
        right = jnp.concatenate(
            [p_vmem[j >> 1, (j & 1) * 2 + m] for m in range(per_row)], axis=1
        )
        left = a_rows[(w >> 5) * nonzeros + (w & 31)]
        return jnp.dot(left, right, preferred_element_type=jnp.float32)

    def second_product(u, i):
        return jnp.dot(pt[i], aps[u][...], preferred_element_type=jnp.float32)

    def entry(g, u):
        v = list_ref[phase, g * UNROLL + u]
        return jnp.maximum((v >> 5) - 1, 0), v & 31

    def keep(u, ap):
        aps[u][...] = ap.astype(jnp.bfloat16)

    def collect(i, k, partial):
        for n in range(per_row):
            to, values = [], []
            for m in range(per_row):
                s = tgt_ref[i, n * nonzeros * per_row + k * per_row + m]
                value = acc[s]
                for other, so_far in zip(to, values):
                    value = jnp.where(s == other, so_far, value)
                to.append(s)
                values.append(
                    value + partial[n * width : (n + 1) * width, m * LANES : (m + 1) * LANES]
                )
            for s, value in zip(to, values):
                acc[s] = value

    def rows_for(g, ready):
        v = list_ref[phase, (g + 1) * UNROLL - 1]
        need = jnp.where(v > 0, v >> 5, rows)
        lax.fori_loop(ready, need, wait_row, 0)
        return jnp.maximum(ready, need)

    def turn(carry):
        g, ready = carry
        ready = rows_for(g + 1, ready)
        held = None
        for u in range(UNROLL):
            i, k = entry(g, u)
            made = u, i, k, second_product(u, i), first_product(g + 1, u)
            if held is not None:
                keep(held[0], held[4])
                collect(*held[1:4])
            held = made
        keep(held[0], held[4])
        collect(*held[1:4])
        return g + 1, ready

    ready = rows_for(0, jnp.int32(0))
    for u in range(UNROLL):
        keep(u, first_product(0, u))
    g, ready = lax.while_loop(
        lambda c: list_ref[phase, (c[0] + 1) * UNROLL] > 0, turn, (jnp.int32(0), ready)
    )
    for u in range(UNROLL):
        i, k = entry(g, u)
        collect(i, k, second_product(u, i))
    lax.fori_loop(ready, rows, wait_row, 0)
    if late:
        for copy in sums:
            copy.wait()

    def total(s):
        value = acc[s]
        for extra in late:
            value = value + extra[s]
        return value

    if last:

        def emit(rz, _):
            for rc in range(2):
                for r in range(members):
                    s = (rz * 2 + (core ^ rc)) * (OWN * members) + r * OWN
                    packed = pack_four([total(s + x) for x in range(OWN)], width)
                    for t in range(3):
                        stages[rc][r, rz, t] = packed[t].astype(stages[rc].dtype)
                copy = pltpu.make_async_copy(stages[rc].at[:, rz], out_refs[rc].at[:, rz], out_sem.at[rc])
                copy.start()
            return 0

        lax.fori_loop(0, groups // 2, emit, 0)
        for rc in range(2):
            pltpu.make_async_copy(stages[rc], out_refs[rc], out_sem.at[rc]).wait()
    else:
        outs = [pltpu.make_async_copy(acc, out_refs[0], out_sem.at[0])]
        if first:
            outs.append(pltpu.make_async_copy(pt, out_refs[1], out_sem.at[1]))
        for copy in outs:
            copy.start()
        for copy in outs:
            copy.wait()


def work(cfg, tables, a_rows, packed, pt=None, sums=()):
    width, rows, nonzeros, per_row = cfg["width"], cfg["rows"], cfg["nonzeros"], cfg["per_row"]
    slots, members, groups = cfg["slots"], cfg["members"], cfg["groups"]
    late = cfg["last"] and cfg["late"]
    cfg = dict(cfg, sources=len(packed), sums=len(sums), late=late)
    quads = sum(x.shape[0] for x in packed)
    operands = [a_rows, *packed] + ([] if cfg["first"] else [pt]) + list(sums)
    pt_shape = (rows, per_row * width, width)
    stages = []
    if cfg["last"]:
        whole = (members, groups // 2, 3, width, LANES)
        shapes = [jax.ShapeDtypeStruct(whole, jnp.float32), jax.ShapeDtypeStruct(whole, jnp.bfloat16)]
        stages = [pltpu.VMEM(x.shape, x.dtype) for x in shapes]
    else:
        shapes = [jax.ShapeDtypeStruct((slots, width, LANES), jnp.float32)]
        if cfg["first"]:
            shapes.append(jax.ShapeDtypeStruct(pt_shape, jnp.bfloat16))
    return pl.pallas_call(
        functools.partial(work_kernel, cfg),
        grid_spec=pltpu.PrefetchScalarGridSpec(
            num_scalar_prefetch=3,
            grid=(),
            in_specs=[HBM] * len(operands),
            out_specs=[HBM] * len(shapes),
            scratch_shapes=[
                pltpu.VMEM((quads, 4, width, LANES), jnp.bfloat16),
                pltpu.VMEM(pt_shape, jnp.bfloat16),
                pltpu.VMEM(((rows + 1) * nonzeros, width, width), jnp.bfloat16),
                pltpu.VMEM((slots, width, LANES), jnp.float32),
            ]
            + [pltpu.VMEM((width, per_row * LANES), jnp.bfloat16)] * UNROLL
            + [
                pltpu.SemaphoreType.DMA((rows,)),
                pltpu.SemaphoreType.DMA((len(packed) + 1 + len(sums),)),
                pltpu.SemaphoreType.DMA((2,)),
            ]
            + stages
            + [pltpu.VMEM((slots, width, LANES), jnp.float32)] * (len(sums) if late else 0),
        ),
        out_shape=shapes,
        compiler_params=pltpu.CompilerParams(vmem_limit_bytes=VMEM_LIMIT),
        cost_estimate=pl.CostEstimate(
            flops=4 * rows * nonzeros * width * width * width,
            bytes_accessed=20_000_000,
            transcendentals=0,
        ),
        name="work_%d" % cfg["phase"],
    )(*tables, *operands)


def make_lists(columns, me, phase_of):
    rows, nonzeros = columns.shape
    entries = rows * nonzeros
    phases = max(phase_of) + 1
    list_len = (-(-entries // UNROLL) + 1) * UNROLL
    relative = ((columns * divider(rows, lax.axis_size("blk"))) >> 16) ^ me
    flat = sum(jnp.where(relative == r, p, 0) for r, p in enumerate(phase_of)).reshape(-1)
    order = jnp.arange(entries, dtype=jnp.int32)
    before = (flat[None, :] == flat[:, None]) & (order[None, :] < order[:, None])
    position = flat * list_len + jnp.sum(before.astype(jnp.int32), axis=1)
    value = (order // nonzeros + 1) * 32 + order % nonzeros
    x = jnp.arange(phases * list_len, dtype=jnp.int32).reshape(phases, list_len)
    found = jnp.where(position[:, None, None] == x[None], value[:, None, None], 0)
    return jnp.sum(found, axis=0)


def shards(a_blocks, col_index, prolong, target):
    rows, nonzeros = a_blocks.shape[1:3]
    per_row = prolong.shape[2]
    width = a_blocks.shape[-1]
    groups = lax.axis_size("grp")
    members = lax.axis_size("blk")
    chips = groups // 2
    slots = groups * OWN * members
    f32, bf16 = jnp.float32, jnp.bfloat16
    me = lax.axis_index("blk").astype(jnp.int32)

    def exchange(x, r, axis="blk", size=members):
        return lax.ppermute(x, axis, [(d, d ^ r) for d in range(size)])

    if members == 4:
        sources = [[0], [1, 2], [3]]
    else:
        sources = [[0]] + [list(range(r, min(r + 3, members))) for r in range(1, members, 3)]
    phases = len(sources)
    phase_of = [p for p in range(phases) for _ in sources[p]]

    own = pack_prolong(prolong)
    packed = [own] + [exchange(own, r) for r in range(1, members)]
    lists = make_lists(col_index[0], me, phase_of)
    cfg = dict(
        width=width, rows=rows, nonzeros=nonzeros, per_row=per_row, slots=slots,
        members=members, groups=groups, late=slots <= 128,
    )
    pt, sums = None, []
    for p in range(phases):
        last = p == phases - 1
        use = [packed[r] for r in sources[p]]
        before = (sums if last else []) if cfg["late"] else sums[-1:]
        outs = work(
            {**cfg, "phase": p, "first": p == 0, "last": last, "from": sources[p][0]},
            (lists, col_index[0], target[0]), a_blocks[0], use, pt, before,
        )
        sums = sums + [outs[0]]
        if p == 0:
            pt = outs[1]

    keep, give = outs
    total = keep + exchange(give, 1, "grp", groups).astype(f32)
    got = lax.all_to_all(total.astype(bf16), "blk", 0, 0, tiled=True)
    total = jnp.sum(got.astype(f32), axis=0)
    same_core = [[c + 2 * z for z in range(chips)] for c in range(2)]
    got = lax.all_to_all(
        total.astype(bf16), "grp", 0, 0, axis_index_groups=same_core, tiled=True
    )
    mine = jnp.sum(got.astype(f32), axis=0)
    fourth = unpack_last([mine[t] for t in range(3)], width)
    return jnp.concatenate([mine[:, :, :width], fourth[None]])[None]


def solution(mesh):
    return jax.shard_map(
        shards,
        mesh=mesh,
        in_specs=(
            P("grp", "blk", None, None, None),
            P("grp", "blk", None),
            P("grp", "blk", None, None, None),
            P("grp", "blk", None),
        ),
        out_specs=P("grp", "blk", None, None),
        check_vma=False,
    )
```

```python
import functools

import jax
import jax.numpy as jnp
from jax import lax
from jax.experimental import pallas as pl
from jax.experimental.pallas import tpu as pltpu
from jax.sharding import PartitionSpec as P

OWN = 4
UNROLL = 16
LANES = 128
AHEAD = 12
VMEM = 64 * 1024 * 1024
HBM = pl.BlockSpec(memory_space=pl.ANY)


def pack_four(blocks, width):
    strip = LANES - width
    return [
        jnp.concatenate(
            [blocks[t][:, :width], blocks[3][:, strip * t : strip * (t + 1)]], axis=1
        )
        for t in range(3)
    ]


def unpack_last(parts, width):
    return jnp.concatenate([part[:, width:] for part in parts], axis=1)


def pack_kernel(p_hbm, *refs):
    out, blocks, packed, in_sem, out_sem = refs
    width, quads = p_hbm.shape[-1], p_hbm.shape[0]
    steps = in_sem.shape[0]
    size = quads // steps
    loads, stores = [], []
    for c in range(steps):
        part = pl.ds(c * size, size)
        loads.append(pltpu.make_async_copy(p_hbm.at[part], blocks.at[part], in_sem.at[c]))
        stores.append(pltpu.make_async_copy(packed.at[part], out.at[part], out_sem.at[c]))
        loads[c].start()
    for c in range(steps):
        loads[c].wait()
        for quad in range(c * size, (c + 1) * size):
            made = pack_four([blocks[quad, t] for t in range(4)], width)
            for t in range(3):
                packed[quad, t] = made[t]
        stores[c].start()
    for store in stores:
        store.wait()


def pack_prolong(prolong):
    width, dtype = prolong.shape[-1], prolong.dtype
    quads = prolong.shape[1] * prolong.shape[2] // 4
    steps = 4
    return pl.pallas_call(
        pack_kernel,
        in_specs=[HBM],
        out_specs=HBM,
        out_shape=jax.ShapeDtypeStruct((quads, 3, width, LANES), dtype),
        scratch_shapes=[
            pltpu.VMEM((quads, 4, width, width), dtype),
            pltpu.VMEM((quads, 3, width, LANES), dtype),
            pltpu.SemaphoreType.DMA((steps,)),
            pltpu.SemaphoreType.DMA((steps,)),
        ],
        compiler_params=pltpu.CompilerParams(vmem_limit_bytes=VMEM // 2),
        name="pack_prolong",
    )(prolong.reshape(quads, 4, width, width))


def divider(rows, members):
    scale = 65536 // rows + 1
    assert all((x * scale) >> 16 == x // rows for x in range(rows * members))
    return scale


def work_kernel(cfg, *refs):
    first, last, phase = cfg["first"], cfg["last"], cfg["phase"]
    width, rows, nonzeros, per_row = cfg["width"], cfg["rows"], cfg["nonzeros"], cfg["per_row"]
    slots, members, groups = cfg["slots"], cfg["members"], cfg["groups"]
    refs = list(refs)
    take = lambda n: [refs.pop(0) for _ in range(n)]
    list_ref, col_ref, tgt_ref, a_hbm = take(4)
    p_hbm = take(cfg["sources"])
    if not first:
        pt, _ = take(2)
    out_refs = take(2 if last else 0)
    (acc,) = take(1)
    if first:
        (pt,) = take(1)
    p_vmem, a_rows = take(2)
    aps = take(UNROLL)
    a_sem, sem, out_sem = take(3)
    stages = take(2 if last else 0)

    me = lax.axis_index("blk").astype(jnp.int32)
    rank = lax.axis_index("grp").astype(jnp.int32)
    chip, core = rank >> 1, rank & 1

    def a_copy(i):
        to = a_rows.at[pl.ds((i + 1) * nonzeros, nonzeros)]
        return pltpu.make_async_copy(a_hbm.at[i], to, a_sem.at[i])

    def start_row(i, _):
        a_copy(i).start()
        return 0

    def wait_row(i, _):
        a_copy(i).wait()

        @pl.when(i + AHEAD < rows)
        def _():
            a_copy(i + AHEAD).start()

        return 0

    p_copies, at = [], 0
    for s, source in enumerate(p_hbm):
        to = p_vmem.at[pl.ds(at, source.shape[0]), pl.ds(0, 3)]
        p_copies.append(pltpu.make_async_copy(source, to, sem.at[s]))
        at += source.shape[0]
    for copy in p_copies:
        copy.start()
    lax.fori_loop(0, AHEAD, start_row, 0)

    a_rows[0] = jnp.zeros((width, width), a_rows.dtype)
    if first:

        def clear(s, _):
            for x in range(8):
                acc[s * 8 + x] = jnp.zeros((width, LANES), acc.dtype)
            return 0

        lax.fori_loop(0, slots // 8, clear, 0)
    for copy in p_copies:
        copy.wait()

    def unpack(q, _):
        for x in range(2):
            parts = [p_vmem[q * 2 + x, t] for t in range(3)]
            p_vmem[q * 2 + x, 3, :, :width] = unpack_last(parts, width)
        return 0

    lax.fori_loop(0, at // 2, unpack, 0)
    if first:

        def transpose(q, _):
            for x in range(4):
                block = p_vmem[q, x].T[:width]
                n = x % per_row
                pt[q * (4 // per_row) + x // per_row, n * width : (n + 1) * width, :] = block
            return 0

        lax.fori_loop(0, at, transpose, 0)
    scale = divider(rows, members)

    def p_block(v):
        j = col_ref[jnp.maximum((v >> 5) - 1, 0), v & 31]
        member = (j * scale) >> 16
        place = ((member ^ me) - cfg["from"]) * rows + j - member * rows
        return jnp.where(v > 0, place, 0)

    def first_product(g, u):
        w = list_ref[phase, g * UNROLL + u]
        j = p_block(w)
        right = jnp.concatenate(
            [p_vmem[j >> 1, (j & 1) * 2 + m] for m in range(per_row)], axis=1
        )
        left = a_rows[(w >> 5) * nonzeros + (w & 31)]
        return jnp.dot(left, right, preferred_element_type=jnp.float32)

    def second_product(u, i):
        return jnp.dot(pt[i], aps[u][...], preferred_element_type=jnp.float32)

    def entry(g, u):
        v = list_ref[phase, g * UNROLL + u]
        return jnp.maximum((v >> 5) - 1, 0), v & 31

    def keep(u, ap):
        aps[u][...] = ap.astype(jnp.bfloat16)

    def collect(i, k, partial):
        for n in range(per_row):
            for m in range(per_row):
                s = tgt_ref[i, n * nonzeros * per_row + k * per_row + m]
                acc[s] = acc[s] + partial[
                    n * width : (n + 1) * width, m * LANES : (m + 1) * LANES
                ]

    def rows_for(g, ready):
        v = list_ref[phase, (g + 1) * UNROLL - 1]
        need = jnp.where(v > 0, v >> 5, rows)
        lax.fori_loop(ready, need, wait_row, 0)
        return jnp.maximum(ready, need)

    def turn(carry):
        g, ready = carry
        ready = rows_for(g + 1, ready)
        held = None
        for u in range(UNROLL):
            i, k = entry(g, u)
            made = u, i, k, second_product(u, i), first_product(g + 1, u)
            if held is not None:
                keep(held[0], held[4])
                collect(*held[1:4])
            held = made
        keep(held[0], held[4])
        collect(*held[1:4])
        return g + 1, ready

    ready = rows_for(0, jnp.int32(0))
    for u in range(UNROLL):
        keep(u, first_product(0, u))
    g, ready = lax.while_loop(
        lambda c: list_ref[phase, (c[0] + 1) * UNROLL] > 0, turn, (jnp.int32(0), ready)
    )
    for u in range(UNROLL):
        i, k = entry(g, u)
        collect(i, k, second_product(u, i))
    lax.fori_loop(ready, rows, wait_row, 0)
    if last:

        def emit(rz, _):
            for rc in range(2):
                for r in range(members):
                    s = ((chip ^ rz) * 2 + (core ^ rc)) * (OWN * members) + (me ^ r) * OWN
                    packed = pack_four([acc[s + x] for x in range(OWN)], width)
                    for t in range(3):
                        stages[rc][rz, r, t] = packed[t].astype(stages[rc].dtype)
                copy = pltpu.make_async_copy(stages[rc].at[rz], out_refs[rc].at[rz], out_sem.at[rc])
                copy.start()
            return 0

        lax.fori_loop(0, groups // 2, emit, 0)
        for rc in range(2):
            pltpu.make_async_copy(stages[rc], out_refs[rc], out_sem.at[rc]).wait()


def work(cfg, tables, a_rows, packed, pt=None, acc=None):
    width, rows, nonzeros, per_row = cfg["width"], cfg["rows"], cfg["nonzeros"], cfg["per_row"]
    slots, members, groups = cfg["slots"], cfg["members"], cfg["groups"]
    first, last = cfg["first"], cfg["last"]
    cfg = dict(cfg, sources=len(packed))
    quads = sum(x.shape[0] for x in packed)
    vmem = pl.BlockSpec(memory_space=pltpu.VMEM)
    operands = [a_rows, *packed]
    in_specs, out_specs = [HBM] * len(operands), [vmem]
    shapes, stages, aliases = [pltpu.VMEM((slots, width, LANES), jnp.float32)], [], {}
    resident = slots * width * LANES * 4 + rows * per_row * width * LANES * 2
    if first:
        shapes.append(pltpu.VMEM((rows, per_row * width, width), jnp.bfloat16))
        out_specs.append(vmem)
    else:
        operands += [pt, acc]
        in_specs += [vmem, vmem]
    if last:
        whole = (groups // 2, members, 3, width, LANES)
        made = [jax.ShapeDtypeStruct(whole, jnp.float32), jax.ShapeDtypeStruct(whole, jnp.bfloat16)]
        stages = [pltpu.VMEM(x.shape, x.dtype) for x in made]
        shapes, out_specs = made + shapes, [HBM] * 2 + out_specs
    if not first:
        aliases = {len(tables) + len(operands) - 1: len(shapes) - 1}
    return pl.pallas_call(
        functools.partial(work_kernel, cfg),
        grid_spec=pltpu.PrefetchScalarGridSpec(
            num_scalar_prefetch=len(tables),
            grid=(),
            in_specs=in_specs,
            out_specs=out_specs,
            scratch_shapes=[
                pltpu.VMEM((quads, 4, width, LANES), jnp.bfloat16),
                pltpu.VMEM(((rows + 1) * nonzeros, width, width), jnp.bfloat16),
            ]
            + [pltpu.VMEM((width, per_row * LANES), jnp.bfloat16)] * UNROLL
            + [
                pltpu.SemaphoreType.DMA((rows,)),
                pltpu.SemaphoreType.DMA((len(packed),)),
                pltpu.SemaphoreType.DMA((2,)),
            ]
            + stages,
        ),
        out_shape=shapes,
        input_output_aliases=aliases,
        compiler_params=pltpu.CompilerParams(vmem_limit_bytes=VMEM - resident - 1024 * 1024),
        cost_estimate=pl.CostEstimate(
            flops=4 * rows * nonzeros * width * width * width,
            bytes_accessed=20_000_000,
            transcendentals=0,
        ),
        name="work_%d" % cfg["phase"],
    )(*tables, *operands)


def make_lists(columns, me, phase_of):
    rows, nonzeros = columns.shape
    entries = rows * nonzeros
    phases = max(phase_of) + 1
    list_len = (-(-entries // UNROLL) + 1) * UNROLL
    relative = ((columns * divider(rows, lax.axis_size("blk"))) >> 16) ^ me
    flat = sum(jnp.where(relative == r, p, 0) for r, p in enumerate(phase_of)).reshape(-1)
    order = jnp.arange(entries, dtype=jnp.int32)
    before = (flat[None, :] == flat[:, None]) & (order[None, :] < order[:, None])
    position = flat * list_len + jnp.sum(before.astype(jnp.int32), axis=1)
    value = (order // nonzeros + 1) * 32 + order % nonzeros
    x = jnp.arange(phases * list_len, dtype=jnp.int32).reshape(phases, list_len)
    found = jnp.where(position[:, None, None] == x[None], value[:, None, None], 0)
    return jnp.sum(found, axis=0)


def shards(a_blocks, col_index, prolong, target):
    rows, nonzeros = a_blocks.shape[1:3]
    per_row = prolong.shape[2]
    width = a_blocks.shape[-1]
    groups = lax.axis_size("grp")
    members = lax.axis_size("blk")
    chips = groups // 2
    slots = groups * OWN * members
    f32, bf16 = jnp.float32, jnp.bfloat16
    me = lax.axis_index("blk").astype(jnp.int32)

    def exchange(x, r, axis="blk", size=members):
        return lax.ppermute(x, axis, [(d, d ^ r) for d in range(size)])

    if members == 4:
        sources = [[0], [1, 2], [3]]
    else:
        sources = [[0]] + [list(range(r, min(r + 3, members))) for r in range(1, members, 3)]
    phases = len(sources)
    phase_of = [p for p in range(phases) for _ in sources[p]]

    own = pack_prolong(prolong)
    packed = [own] + [exchange(own, r) for r in range(1, members)]
    lists = make_lists(col_index[0], me, phase_of)
    cfg = dict(
        width=width, rows=rows, nonzeros=nonzeros, per_row=per_row, slots=slots,
        members=members, groups=groups,
    )
    pt = acc = None
    for p in range(phases):
        outs = work(
            {**cfg, "phase": p, "first": p == 0, "last": p == phases - 1, "from": sources[p][0]},
            (lists, col_index[0], target[0]), a_blocks[0], [packed[r] for r in sources[p]], pt, acc,
        )
        if p == 0:
            acc, pt = outs
        elif p < phases - 1:
            (acc,) = outs

    keep, give = outs[:2]
    total = keep + exchange(give, 1, "grp", groups).astype(f32)
    got = [exchange(total[:, r].astype(bf16), r) for r in range(1, members)]
    total = total[:, 0]
    for part in got:
        total = total + part.astype(f32)
    got = [exchange(total[r].astype(bf16), 2 * r, "grp", groups) for r in range(1, chips)]
    mine = total[0]
    for part in got:
        mine = mine + part.astype(f32)
    fourth = unpack_last([mine[t] for t in range(3)], width)
    return jnp.concatenate([mine[:, :, :width], fourth[None]])[None]


def solution(mesh):
    return jax.shard_map(
        shards,
        mesh=mesh,
        in_specs=(
            P("grp", "blk", None, None, None),
            P("grp", "blk", None),
            P("grp", "blk", None, None, None),
            P("grp", "blk", None),
        ),
        out_specs=P("grp", "blk", None, None),
        check_vma=False,
    )
```

```python
import functools

import jax
import jax.numpy as jnp
from jax import lax
from jax.experimental import pallas as pl
from jax.experimental.pallas import tpu as pltpu
from jax.sharding import PartitionSpec as P

OWN = 4
UNROLL = 24
LANES = 128
AHEAD = 12
VMEM = 64 * 1024 * 1024
HBM = pl.BlockSpec(memory_space=pl.ANY)


def pack_four(blocks, width):
    strip = LANES - width
    return [
        jnp.concatenate(
            [blocks[t][:, :width], blocks[3][:, strip * t : strip * (t + 1)]], axis=1
        )
        for t in range(3)
    ]


def unpack_last(parts, width):
    return jnp.concatenate([part[:, width:] for part in parts], axis=1)


def pack_kernel(p_hbm, *refs):
    out, blocks, packed, in_sem, out_sem = refs
    width, quads = p_hbm.shape[-1], p_hbm.shape[0]
    steps = in_sem.shape[0]
    size = quads // steps
    loads, stores = [], []
    for c in range(steps):
        part = pl.ds(c * size, size)
        loads.append(pltpu.make_async_copy(p_hbm.at[part], blocks.at[part], in_sem.at[c]))
        stores.append(pltpu.make_async_copy(packed.at[part], out.at[part], out_sem.at[c]))
        loads[c].start()
    for c in range(steps):
        loads[c].wait()
        for quad in range(c * size, (c + 1) * size):
            made = pack_four([blocks[quad, t] for t in range(4)], width)
            for t in range(3):
                packed[quad, t] = made[t]
        stores[c].start()
    for store in stores:
        store.wait()


def pack_prolong(prolong):
    width, dtype = prolong.shape[-1], prolong.dtype
    quads = prolong.shape[1] * prolong.shape[2] // 4
    steps = 4
    return pl.pallas_call(
        pack_kernel,
        in_specs=[HBM],
        out_specs=HBM,
        out_shape=jax.ShapeDtypeStruct((quads, 3, width, LANES), dtype),
        scratch_shapes=[
            pltpu.VMEM((quads, 4, width, width), dtype),
            pltpu.VMEM((quads, 3, width, LANES), dtype),
            pltpu.SemaphoreType.DMA((steps,)),
            pltpu.SemaphoreType.DMA((steps,)),
        ],
        compiler_params=pltpu.CompilerParams(vmem_limit_bytes=VMEM - 128 * 1024),
        name="pack_prolong",
    )(prolong.reshape(quads, 4, width, width))


def divider(rows, members):
    scale = 65536 // rows + 1
    assert all((x * scale) >> 16 == x // rows for x in range(rows * members))
    return scale


def work_kernel(cfg, *refs):
    first, last, phase = cfg["first"], cfg["last"], cfg["phase"]
    width, rows, nonzeros, per_row = cfg["width"], cfg["rows"], cfg["nonzeros"], cfg["per_row"]
    slots, members, groups = cfg["slots"], cfg["members"], cfg["groups"]
    refs = list(refs)
    take = lambda n: [refs.pop(0) for _ in range(n)]
    list_ref, col_ref, tgt_ref, a_hbm = take(4)
    p_hbm = take(cfg["sources"])
    take(0 if first else 2)
    out_refs = take(2 if last else 0)
    acc, pt = take(2)
    p_vmem, a_rows = take(2)
    aps = take(UNROLL)
    a_sem, sem, out_sem = take(3)
    stages = take(2 if last else 0)

    me = lax.axis_index("blk").astype(jnp.int32)
    rank = lax.axis_index("grp").astype(jnp.int32)
    chip, core = rank >> 1, rank & 1

    def a_copy(i):
        to = a_rows.at[pl.ds((i + 1) * nonzeros, nonzeros)]
        return pltpu.make_async_copy(a_hbm.at[i], to, a_sem.at[i])

    def start_row(i, _):
        a_copy(i).start()
        return 0

    def wait_row(i, _):
        a_copy(i).wait()

        @pl.when(i + AHEAD < rows)
        def _():
            a_copy(i + AHEAD).start()

        return 0

    p_copies, at = [], 0
    for s, source in enumerate(p_hbm):
        to = p_vmem.at[pl.ds(at, source.shape[0]), pl.ds(0, 3)]
        p_copies.append(pltpu.make_async_copy(source, to, sem.at[s]))
        at += source.shape[0]
    for copy in p_copies:
        copy.start()
    lax.fori_loop(0, AHEAD, start_row, 0)

    a_rows[0] = jnp.zeros((width, width), a_rows.dtype)
    if first:

        def clear(s, _):
            for x in range(8):
                acc[s * 8 + x] = jnp.zeros((width, LANES), acc.dtype)
            return 0

        lax.fori_loop(0, slots // 8, clear, 0)
    for copy in p_copies:
        copy.wait()

    def unpack(q, _):
        for x in range(2):
            parts = [p_vmem[q * 2 + x, t] for t in range(3)]
            p_vmem[q * 2 + x, 3, :, :width] = unpack_last(parts, width)
        return 0

    lax.fori_loop(0, at // 2, unpack, 0)
    if first:

        def transpose(q, _):
            for x in range(4):
                block = p_vmem[q, x].T[:width]
                n = x % per_row
                pt[q * (4 // per_row) + x // per_row, n * width : (n + 1) * width, :] = block
            return 0

        lax.fori_loop(0, at, transpose, 0)
    scale = divider(rows, members)

    def p_block(v):
        j = col_ref[jnp.maximum((v >> 5) - 1, 0), v & 31]
        member = (j * scale) >> 16
        place = ((member ^ me) - cfg["from"]) * rows + j - member * rows
        return jnp.where(v > 0, place, 0)

    def first_product(g, u):
        w = list_ref[phase, g * UNROLL + u]
        j = p_block(w)
        right = jnp.concatenate(
            [p_vmem[j >> 1, (j & 1) * 2 + m] for m in range(per_row)], axis=1
        )
        left = a_rows[(w >> 5) * nonzeros + (w & 31)]
        return jnp.dot(left, right, preferred_element_type=jnp.float32)

    def second_product(u, i):
        return jnp.dot(pt[i], aps[u][...], preferred_element_type=jnp.float32)

    def entry(g, u):
        v = list_ref[phase, g * UNROLL + u]
        return jnp.maximum((v >> 5) - 1, 0), v & 31

    def keep(u, ap):
        aps[u][...] = ap.astype(jnp.bfloat16)

    def collect(i, k, partial):
        for n in range(per_row):
            for m in range(per_row):
                s = tgt_ref[i, n * nonzeros * per_row + k * per_row + m]
                acc[s] = acc[s] + partial[
                    n * width : (n + 1) * width, m * LANES : (m + 1) * LANES
                ]

    def rows_for(g, ready):
        v = list_ref[phase, (g + 1) * UNROLL - 1]
        need = jnp.where(v > 0, v >> 5, rows)
        lax.fori_loop(ready, need, wait_row, 0)
        return jnp.maximum(ready, need)

    def turn(carry):
        g, ready = carry
        ready = rows_for(g + 1, ready)
        held = None
        for u in range(UNROLL):
            i, k = entry(g, u)
            made = u, i, k, second_product(u, i), first_product(g + 1, u)
            if held is not None:
                keep(held[0], held[4])
                collect(*held[1:4])
            held = made
        keep(held[0], held[4])
        collect(*held[1:4])
        return g + 1, ready

    ready = rows_for(0, jnp.int32(0))
    for u in range(UNROLL):
        keep(u, first_product(0, u))
    g, ready = lax.while_loop(
        lambda c: list_ref[phase, (c[0] + 1) * UNROLL] > 0, turn, (jnp.int32(0), ready)
    )
    for u in range(UNROLL):
        i, k = entry(g, u)
        collect(i, k, second_product(u, i))
    lax.fori_loop(ready, rows, wait_row, 0)
    if last:

        def emit(rz, _):
            for rc in range(2):
                for r in range(members):
                    s = ((chip ^ rz) * 2 + (core ^ rc)) * (OWN * members) + (me ^ r) * OWN
                    packed = pack_four([acc[s + x] for x in range(OWN)], width)
                    for t in range(3):
                        stages[rc][rz, r, t] = packed[t].astype(stages[rc].dtype)
                copy = pltpu.make_async_copy(stages[rc].at[rz], out_refs[rc].at[rz], out_sem.at[rc])
                copy.start()
            return 0

        lax.fori_loop(0, groups // 2, emit, 0)
        for rc in range(2):
            pltpu.make_async_copy(stages[rc], out_refs[rc], out_sem.at[rc]).wait()


def work(cfg, tables, a_rows, packed, acc=None, pt=None):
    width, rows, nonzeros, per_row = cfg["width"], cfg["rows"], cfg["nonzeros"], cfg["per_row"]
    slots, members, groups = cfg["slots"], cfg["members"], cfg["groups"]
    first, last = cfg["first"], cfg["last"]
    cfg = dict(cfg, sources=len(packed))
    quads = sum(x.shape[0] for x in packed)
    vmem = pl.BlockSpec(memory_space=pltpu.VMEM)
    operands = [a_rows, *packed]
    in_specs, out_specs = [HBM] * len(operands), [vmem] * 2
    shapes, stages, aliases = [
        pltpu.VMEM((slots, width, LANES), jnp.float32),
        pltpu.VMEM((rows, per_row * width, width), jnp.bfloat16),
    ], [], {}
    resident = slots * width * LANES * 4 + rows * per_row * width * LANES * 2
    if not first:
        operands += [acc, pt]
        in_specs += [vmem] * 2
    if last:
        whole = (groups // 2, members, 3, width, LANES)
        made = [jax.ShapeDtypeStruct(whole, jnp.float32), jax.ShapeDtypeStruct(whole, jnp.bfloat16)]
        stages = [pltpu.VMEM(x.shape, x.dtype) for x in made]
        shapes, out_specs = made + shapes, [HBM] * 2 + out_specs
    if not first:
        aliases = {len(tables) + len(operands) - x: len(shapes) - x for x in (1, 2)}
    return pl.pallas_call(
        functools.partial(work_kernel, cfg),
        grid_spec=pltpu.PrefetchScalarGridSpec(
            num_scalar_prefetch=len(tables),
            grid=(),
            in_specs=in_specs,
            out_specs=out_specs,
            scratch_shapes=[
                pltpu.VMEM((quads, 4, width, LANES), jnp.bfloat16),
                pltpu.VMEM(((rows + 1) * nonzeros, width, width), jnp.bfloat16),
            ]
            + [pltpu.VMEM((width, per_row * LANES), jnp.bfloat16)] * UNROLL
            + [
                pltpu.SemaphoreType.DMA((rows,)),
                pltpu.SemaphoreType.DMA((len(packed),)),
                pltpu.SemaphoreType.DMA((2,)),
            ]
            + stages,
        ),
        out_shape=shapes,
        input_output_aliases=aliases,
        compiler_params=pltpu.CompilerParams(vmem_limit_bytes=VMEM - resident - 1024 * 1024),
        cost_estimate=pl.CostEstimate(
            flops=4 * rows * nonzeros * width * width * width,
            bytes_accessed=20_000_000,
            transcendentals=0,
        ),
        name="work_%d" % cfg["phase"],
    )(*tables, *operands)


def make_lists(columns, me, phase_of):
    rows, nonzeros = columns.shape
    entries = rows * nonzeros
    phases = max(phase_of) + 1
    list_len = (-(-entries // UNROLL) + 1) * UNROLL
    relative = ((columns * divider(rows, lax.axis_size("blk"))) >> 16) ^ me
    flat = sum(jnp.where(relative == r, p, 0) for r, p in enumerate(phase_of)).reshape(-1)
    order = jnp.arange(entries, dtype=jnp.int32)
    before = (flat[None, :] == flat[:, None]) & (order[None, :] < order[:, None])
    position = flat * list_len + jnp.sum(before.astype(jnp.int32), axis=1)
    value = (order // nonzeros + 1) * 32 + order % nonzeros
    x = jnp.arange(phases * list_len, dtype=jnp.int32).reshape(phases, list_len)
    found = jnp.where(position[:, None, None] == x[None], value[:, None, None], 0)
    return jnp.sum(found, axis=0)


def shards(a_blocks, col_index, prolong, target):
    rows, nonzeros = a_blocks.shape[1:3]
    per_row = prolong.shape[2]
    width = a_blocks.shape[-1]
    groups = lax.axis_size("grp")
    members = lax.axis_size("blk")
    chips = groups // 2
    slots = groups * OWN * members
    f32, bf16 = jnp.float32, jnp.bfloat16
    me = lax.axis_index("blk").astype(jnp.int32)

    def exchange(x, r, axis="blk", size=members):
        return lax.ppermute(x, axis, [(d, d ^ r) for d in range(size)])

    if members == 4:
        sources = [[0], [1, 2], [3]]
    else:
        sources = [[0]] + [list(range(r, min(r + 3, members))) for r in range(1, members, 3)]
    phases = len(sources)
    phase_of = [p for p in range(phases) for _ in sources[p]]

    own = pack_prolong(prolong)
    packed = [own] + [exchange(own, r) for r in range(1, members)]
    lists = make_lists(col_index[0], me, phase_of)
    cfg = dict(
        width=width, rows=rows, nonzeros=nonzeros, per_row=per_row, slots=slots,
        members=members, groups=groups,
    )
    acc = pt = None
    for p in range(phases):
        outs = work(
            {**cfg, "phase": p, "first": p == 0, "last": p == phases - 1, "from": sources[p][0]},
            (lists, col_index[0], target[0]), a_blocks[0], [packed[r] for r in sources[p]], acc, pt,
        )
        acc, pt = outs[-2:]

    keep, give = outs[:2]
    total = keep + exchange(give, 1, "grp", groups).astype(f32)
    got = [exchange(total[:, r].astype(bf16), r) for r in range(1, members)]
    total = total[:, 0]
    for part in got:
        total = total + part.astype(f32)
    got = [exchange(total[r].astype(bf16), 2 * r, "grp", groups) for r in range(1, chips)]
    mine = total[0]
    for part in got:
        mine = mine + part.astype(f32)
    fourth = unpack_last([mine[t] for t in range(3)], width)
    return jnp.concatenate([mine[:, :, :width], fourth[None]])[None]


def solution(mesh):
    return jax.shard_map(
        shards,
        mesh=mesh,
        in_specs=(
            P("grp", "blk", None, None, None),
            P("grp", "blk", None),
            P("grp", "blk", None, None, None),
            P("grp", "blk", None),
        ),
        out_specs=P("grp", "blk", None, None),
        check_vma=False,
    )
```

```python
import functools

import jax
import jax.numpy as jnp
from jax import lax
from jax.experimental import pallas as pl
from jax.experimental.pallas import tpu as pltpu
from jax.sharding import PartitionSpec as P

OWN = 4
UNROLL = 32
LANES = 128
CHUNK = 3
AHEAD = 4
VMEM = 64 * 1024 * 1024
HBM = pl.BlockSpec(memory_space=pl.ANY)


def pack_four(blocks, width):
    strip = LANES - width
    return [
        jnp.concatenate(
            [blocks[t][:, :width], blocks[3][:, strip * t : strip * (t + 1)]], axis=1
        )
        for t in range(3)
    ]


def unpack_last(parts, width):
    return jnp.concatenate([part[:, width:] for part in parts], axis=1)


def pack_kernel(p_hbm, *refs):
    outs, (blocks, packed, in_sem, out_sem) = refs[:2], refs[2:]
    width, quads = p_hbm.shape[-1], p_hbm.shape[0]
    steps = in_sem.shape[0]
    size = quads // steps
    half = steps // 2
    loads, stores = [], []
    for c in range(steps):
        part = pl.ds(c * size, size)
        to = outs[c // half].at[pl.ds(c % half * size, size)]
        loads.append(pltpu.make_async_copy(p_hbm.at[part], blocks.at[part], in_sem.at[c]))
        stores.append(pltpu.make_async_copy(packed.at[part], to, out_sem.at[c]))
        loads[c].start()
    for c in range(steps):
        loads[c].wait()
        for quad in range(c * size, (c + 1) * size):
            made = pack_four([blocks[quad, t] for t in range(4)], width)
            for t in range(3):
                packed[quad, t] = made[t]
        stores[c].start()
    for store in stores:
        store.wait()


def pack_prolong(prolong):
    width, dtype = prolong.shape[-1], prolong.dtype
    quads = prolong.shape[1] * prolong.shape[2] // 4
    steps = 4
    return pl.pallas_call(
        pack_kernel,
        in_specs=[HBM],
        out_specs=[HBM] * 2,
        out_shape=[jax.ShapeDtypeStruct((quads // 2, 3, width, LANES), dtype)] * 2,
        scratch_shapes=[
            pltpu.VMEM((quads, 4, width, width), dtype),
            pltpu.VMEM((quads, 3, width, LANES), dtype),
            pltpu.SemaphoreType.DMA((steps,)),
            pltpu.SemaphoreType.DMA((steps,)),
        ],
        compiler_params=pltpu.CompilerParams(vmem_limit_bytes=VMEM - 128 * 1024),
        name="pack_prolong",
    )(prolong.reshape(quads, 4, width, width))


def divider(rows, members):
    scale = 65536 // rows + 1
    assert all((x * scale) >> 16 == x // rows for x in range(rows * members))
    return scale


def work_kernel(cfg, *refs):
    first, last, phase = cfg["first"], cfg["last"], cfg["phase"]
    width, rows, nonzeros, per_row = cfg["width"], cfg["rows"], cfg["nonzeros"], cfg["per_row"]
    slots, members, groups = cfg["slots"], cfg["members"], cfg["groups"]
    refs = list(refs)
    take = lambda n: [refs.pop(0) for _ in range(n)]
    list_ref, col_ref, tgt_ref, a_hbm = take(4)
    p_hbm = take(cfg["sources"])
    take(0 if first else 2)
    out_refs = take(2 if last else 0)
    acc, pt = take(2)
    p_vmem, a_rows = take(2)
    aps = take(UNROLL)
    a_sem, sem, out_sem = take(3)
    stages = take(2 if last else 0)

    me = lax.axis_index("blk").astype(jnp.int32)
    rank = lax.axis_index("grp").astype(jnp.int32)
    chip, core = rank >> 1, rank & 1

    chunks = rows // CHUNK

    def a_copy(c):
        blocks = CHUNK * nonzeros
        to = a_rows.at[pl.ds(nonzeros + c * blocks, blocks)]
        return pltpu.make_async_copy(a_hbm.at[pl.ds(c * blocks, blocks)], to, a_sem.at[c])

    def start_chunk(c, _):
        a_copy(c).start()
        return 0

    def wait_chunk(c, _):
        a_copy(c).wait()

        @pl.when(c + AHEAD < chunks)
        def _():
            a_copy(c + AHEAD).start()

        return 0

    p_copies, at = [], 0
    for s, source in enumerate(p_hbm):
        to = p_vmem.at[pl.ds(at, source.shape[0]), pl.ds(0, 3)]
        p_copies.append(pltpu.make_async_copy(source, to, sem.at[s]))
        at += source.shape[0]
    for copy in p_copies:
        copy.start()
    lax.fori_loop(0, AHEAD, start_chunk, 0)

    a_rows[0] = jnp.zeros((width, width), a_rows.dtype)
    if first:

        def clear(s, _):
            for x in range(8):
                acc[s * 8 + x] = jnp.zeros((width, LANES), acc.dtype)
            return 0

        lax.fori_loop(0, slots // 8, clear, 0)
    for copy in p_copies:
        copy.wait()

    def unpack(q, _):
        for x in range(2):
            parts = [p_vmem[q * 2 + x, t] for t in range(3)]
            p_vmem[q * 2 + x, 3, :, :width] = unpack_last(parts, width)
        return 0

    lax.fori_loop(0, at // 2, unpack, 0)
    if first:

        def transpose(q, _):
            for x in range(4):
                block = p_vmem[q, x].T[:width]
                n = x % per_row
                pt[q * (4 // per_row) + x // per_row, n * width : (n + 1) * width, :] = block
            return 0

        lax.fori_loop(0, at, transpose, 0)
    scale = divider(rows, members)

    def p_block(v):
        j = col_ref[jnp.maximum((v >> 5) - 1, 0), v & 31]
        member = (j * scale) >> 16
        place = ((member ^ me) - cfg["from"]) * rows + j - member * rows
        return jnp.where(v > 0, place, 0)

    def first_product(g, u):
        w = list_ref[phase, g * UNROLL + u]
        j = p_block(w)
        right = jnp.concatenate(
            [p_vmem[j >> 1, (j & 1) * 2 + m] for m in range(per_row)], axis=1
        )
        left = a_rows[(w >> 5) * nonzeros + (w & 31)]
        return jnp.dot(left, right, preferred_element_type=jnp.float32)

    def second_product(u, i):
        return jnp.dot(pt[i], aps[u][...], preferred_element_type=jnp.float32)

    def entry(g, u):
        v = list_ref[phase, g * UNROLL + u]
        return jnp.maximum((v >> 5) - 1, 0), v & 31

    def keep(u, ap):
        aps[u][...] = ap.astype(jnp.bfloat16)

    def collect(i, k, partial):
        for n in range(per_row):
            for m in range(per_row):
                s = tgt_ref[i, n * nonzeros * per_row + k * per_row + m]
                acc[s] = acc[s] + partial[
                    n * width : (n + 1) * width, m * LANES : (m + 1) * LANES
                ]

    def rows_for(g, ready):
        v = list_ref[phase, (g + 1) * UNROLL - 1]
        whole = divider(CHUNK, rows // CHUNK + 1)
        need = jnp.where(v > 0, ((v >> 5) + CHUNK - 1) * whole >> 16, chunks)
        lax.fori_loop(ready, need, wait_chunk, 0)
        return jnp.maximum(ready, need)

    def turn(carry):
        g, ready = carry
        ready = rows_for(g + 1, ready)
        held = None
        for u in range(UNROLL):
            i, k = entry(g, u)
            made = u, i, k, second_product(u, i), first_product(g + 1, u)
            if held is not None:
                keep(held[0], held[4])
                collect(*held[1:4])
            held = made
        keep(held[0], held[4])
        collect(*held[1:4])
        return g + 1, ready

    ready = rows_for(0, jnp.int32(0))
    for u in range(UNROLL):
        keep(u, first_product(0, u))
    g, ready = lax.while_loop(
        lambda c: list_ref[phase, (c[0] + 1) * UNROLL] > 0, turn, (jnp.int32(0), ready)
    )
    for u in range(UNROLL):
        i, k = entry(g, u)
        collect(i, k, second_product(u, i))
    lax.fori_loop(ready, chunks, wait_chunk, 0)
    if last:

        def emit(rz, _):
            for rc in range(2):
                for r in range(members):
                    s = ((chip ^ rz) * 2 + (core ^ rc)) * (OWN * members) + (me ^ r) * OWN
                    packed = pack_four([acc[s + x] for x in range(OWN)], width)
                    for t in range(3):
                        stages[rc][rz, r, t] = packed[t].astype(stages[rc].dtype)
                copy = pltpu.make_async_copy(stages[rc].at[rz], out_refs[rc].at[rz], out_sem.at[rc])
                copy.start()
            return 0

        lax.fori_loop(0, groups // 2, emit, 0)
        for rc in range(2):
            pltpu.make_async_copy(stages[rc], out_refs[rc], out_sem.at[rc]).wait()


def work(cfg, tables, a_rows, packed, acc=None, pt=None):
    width, rows, nonzeros, per_row = cfg["width"], cfg["rows"], cfg["nonzeros"], cfg["per_row"]
    slots, members, groups = cfg["slots"], cfg["members"], cfg["groups"]
    first, last = cfg["first"], cfg["last"]
    cfg = dict(cfg, sources=len(packed))
    quads = sum(x.shape[0] for x in packed)
    vmem = pl.BlockSpec(memory_space=pltpu.VMEM)
    operands = [a_rows.reshape(rows * nonzeros, width, width), *packed]
    in_specs, out_specs = [HBM] * len(operands), [vmem] * 2
    shapes, stages, aliases = [
        pltpu.VMEM((slots, width, LANES), jnp.float32),
        pltpu.VMEM((rows, per_row * width, width), jnp.bfloat16),
    ], [], {}
    resident = slots * width * LANES * 4 + rows * per_row * width * LANES * 2
    if not first:
        operands += [acc, pt]
        in_specs += [vmem] * 2
    if last:
        whole = (groups // 2, members, 3, width, LANES)
        made = [jax.ShapeDtypeStruct(whole, jnp.float32), jax.ShapeDtypeStruct(whole, jnp.bfloat16)]
        stages = [pltpu.VMEM(x.shape, x.dtype) for x in made]
        shapes, out_specs = made + shapes, [HBM] * 2 + out_specs
    if not first:
        aliases = {len(tables) + len(operands) - x: len(shapes) - x for x in (1, 2)}
    return pl.pallas_call(
        functools.partial(work_kernel, cfg),
        grid_spec=pltpu.PrefetchScalarGridSpec(
            num_scalar_prefetch=len(tables),
            grid=(),
            in_specs=in_specs,
            out_specs=out_specs,
            scratch_shapes=[
                pltpu.VMEM((quads, 4, width, LANES), jnp.bfloat16),
                pltpu.VMEM(((rows + 1) * nonzeros, width, width), jnp.bfloat16),
            ]
            + [pltpu.VMEM((width, per_row * LANES), jnp.bfloat16)] * UNROLL
            + [
                pltpu.SemaphoreType.DMA((rows // CHUNK,)),
                pltpu.SemaphoreType.DMA((len(packed),)),
                pltpu.SemaphoreType.DMA((2,)),
            ]
            + stages,
        ),
        out_shape=shapes,
        input_output_aliases=aliases,
        compiler_params=pltpu.CompilerParams(vmem_limit_bytes=VMEM - resident - 256 * 1024),
        cost_estimate=pl.CostEstimate(
            flops=4 * rows * nonzeros * width * width * width,
            bytes_accessed=20_000_000,
            transcendentals=0,
        ),
        name="work_%d" % cfg["phase"],
    )(*tables, *operands)


def make_lists(columns, me, phase_of):
    rows, nonzeros = columns.shape
    entries = rows * nonzeros
    phases = max(phase_of) + 1
    list_len = (-(-entries // UNROLL) + 1) * UNROLL
    relative = ((columns * divider(rows, lax.axis_size("blk"))) >> 16) ^ me
    flat = sum(jnp.where(relative == r, p, 0) for r, p in enumerate(phase_of)).reshape(-1)
    order = jnp.arange(entries, dtype=jnp.int32)
    before = (flat[None, :] == flat[:, None]) & (order[None, :] < order[:, None])
    position = flat * list_len + jnp.sum(before.astype(jnp.int32), axis=1)
    value = (order // nonzeros + 1) * 32 + order % nonzeros
    x = jnp.arange(phases * list_len, dtype=jnp.int32).reshape(phases, list_len)
    found = jnp.where(position[:, None, None] == x[None], value[:, None, None], 0)
    return jnp.sum(found, axis=0)


def shards(a_blocks, col_index, prolong, target):
    rows, nonzeros = a_blocks.shape[1:3]
    per_row = prolong.shape[2]
    width = a_blocks.shape[-1]
    groups = lax.axis_size("grp")
    members = lax.axis_size("blk")
    chips = groups // 2
    slots = groups * OWN * members
    f32, bf16 = jnp.float32, jnp.bfloat16
    me = lax.axis_index("blk").astype(jnp.int32)

    def exchange(x, r, axis="blk", size=members):
        return lax.ppermute(x, axis, [(d, d ^ r) for d in range(size)])

    if members == 4:
        sources = [[0], [1, 2], [3]]
    else:
        sources = [[0]] + [list(range(r, min(r + 3, members))) for r in range(1, members, 3)]
    phases = len(sources)
    phase_of = [p for p in range(phases) for _ in sources[p]]

    own = pack_prolong(prolong)
    direct = range(1, 3 if members == 4 else members)
    packed = {0: own, **{r: [exchange(x, r) for x in own] for r in direct}}
    lists = make_lists(col_index[0], me, phase_of)
    cfg = dict(
        width=width, rows=rows, nonzeros=nonzeros, per_row=per_row, slots=slots,
        members=members, groups=groups,
    )
    acc = pt = None
    for p in range(phases):
        outs = work(
            {**cfg, "phase": p, "first": p == 0, "last": p == phases - 1, "from": sources[p][0]},
            (lists, col_index[0], target[0]), a_blocks[0], [x for r in sources[p] for x in packed[r]], acc, pt,
        )
        acc, pt = outs[-2:]
        if p == 0 and members == 4:
            near, acc = lax.optimization_barrier((packed[1] + packed[2], acc))
            packed = {0: own, 1: near[:2], 2: near[2:]}
            packed[3] = [exchange(near[0], 2), exchange(near[3], 1)]

    keep, give = outs[:2]
    total = keep + exchange(give, 1, "grp", groups).astype(f32)
    got = [exchange(total[:, r].astype(bf16), r) for r in range(1, members)]
    total = total[:, 0]
    for part in got:
        total = total + part.astype(f32)
    got = [exchange(total[r].astype(bf16), 2 * r, "grp", groups) for r in range(1, chips)]
    mine = total[0]
    for part in got:
        mine = mine + part.astype(f32)
    fourth = unpack_last([mine[t] for t in range(3)], width)
    return jnp.concatenate([mine[:, :, :width], fourth[None]])[None]


def solution(mesh):
    return jax.shard_map(
        shards,
        mesh=mesh,
        in_specs=(
            P("grp", "blk", None, None, None),
            P("grp", "blk", None),
            P("grp", "blk", None, None, None),
            P("grp", "blk", None),
        ),
        out_specs=P("grp", "blk", None, None),
        check_vma=False,
    )
```

```python
import functools

import jax
import jax.numpy as jnp
from jax import lax
from jax.experimental import pallas as pl
from jax.experimental.pallas import tpu as pltpu
from jax.sharding import PartitionSpec as P

OWN = 4
UNROLL = 32
LANES = 128
CHUNK = 3
AHEAD = 4
VMEM = 64 * 1024 * 1024
HBM = pl.BlockSpec(memory_space=pl.ANY)


def pack_four(blocks, width):
    strip = LANES - width
    return [
        jnp.concatenate(
            [blocks[t][:, :width], blocks[3][:, strip * t : strip * (t + 1)]], axis=1
        )
        for t in range(3)
    ]


def unpack_last(parts, width):
    return jnp.concatenate([part[:, width:] for part in parts], axis=1)


def pack_kernel(p_hbm, *refs):
    outs, (blocks, packed, in_sem, out_sem) = refs[:2], refs[2:]
    width, quads = p_hbm.shape[-1], p_hbm.shape[0]
    steps = in_sem.shape[0]
    size = quads // steps
    half = steps // 2
    loads, stores = [], []
    for c in range(steps):
        part = pl.ds(c * size, size)
        to = outs[c // half].at[pl.ds(c % half * size, size)]
        loads.append(pltpu.make_async_copy(p_hbm.at[part], blocks.at[part], in_sem.at[c]))
        stores.append(pltpu.make_async_copy(packed.at[part], to, out_sem.at[c]))
        loads[c].start()
    for c in range(steps):
        loads[c].wait()
        for quad in range(c * size, (c + 1) * size):
            made = pack_four([blocks[quad, t] for t in range(4)], width)
            for t in range(3):
                packed[quad, t] = made[t]
        stores[c].start()
    for store in stores:
        store.wait()


def pack_prolong(prolong):
    width, dtype = prolong.shape[-1], prolong.dtype
    quads = prolong.shape[1] * prolong.shape[2] // 4
    steps = 4
    return pl.pallas_call(
        pack_kernel,
        in_specs=[HBM],
        out_specs=[HBM] * 2,
        out_shape=[jax.ShapeDtypeStruct((quads // 2, 3, width, LANES), dtype)] * 2,
        scratch_shapes=[
            pltpu.VMEM((quads, 4, width, width), dtype),
            pltpu.VMEM((quads, 3, width, LANES), dtype),
            pltpu.SemaphoreType.DMA((steps,)),
            pltpu.SemaphoreType.DMA((steps,)),
        ],
        compiler_params=pltpu.CompilerParams(vmem_limit_bytes=VMEM - 128 * 1024),
        name="pack_prolong",
    )(prolong.reshape(quads, 4, width, width))


def divider(rows, members):
    scale = 65536 // rows + 1
    assert all((x * scale) >> 16 == x // rows for x in range(rows * members))
    return scale


def work_kernel(cfg, *refs):
    first, last, phase = cfg["first"], cfg["last"], cfg["phase"]
    width, rows, nonzeros, per_row = cfg["width"], cfg["rows"], cfg["nonzeros"], cfg["per_row"]
    slots, members, groups = cfg["slots"], cfg["members"], cfg["groups"]
    refs = list(refs)
    take = lambda n: [refs.pop(0) for _ in range(n)]
    list_ref, col_ref, tgt_ref, a_hbm = take(4)
    p_hbm = take(cfg["sources"])
    take(0 if first else 2)
    give_out = take(1 if last else 0)
    acc, pt = take(2)
    p_vmem, a_rows = take(2)
    aps = take(UNROLL)
    a_sem, sem, out_sem = take(3)
    stages = take(1 if last else 0)

    me = lax.axis_index("blk").astype(jnp.int32)

    chunks = rows // CHUNK

    def a_copy(c):
        blocks = CHUNK * nonzeros
        to = a_rows.at[pl.ds(nonzeros + c * blocks, blocks)]
        return pltpu.make_async_copy(a_hbm.at[pl.ds(c * blocks, blocks)], to, a_sem.at[c])

    def start_chunk(c, _):
        a_copy(c).start()
        return 0

    def wait_chunk(c, _):
        a_copy(c).wait()

        @pl.when(c + AHEAD < chunks)
        def _():
            a_copy(c + AHEAD).start()

        return 0

    p_copies, at = [], 0
    for s, source in enumerate(p_hbm):
        to = p_vmem.at[pl.ds(at, source.shape[0]), pl.ds(0, 3)]
        p_copies.append(pltpu.make_async_copy(source, to, sem.at[s]))
        at += source.shape[0]
    for copy in p_copies:
        copy.start()
    lax.fori_loop(0, AHEAD, start_chunk, 0)

    a_rows[0] = jnp.zeros((width, width), a_rows.dtype)
    if first:

        def clear(s, _):
            for x in range(8):
                acc[s * 8 + x] = jnp.zeros((width, LANES), acc.dtype)
            return 0

        lax.fori_loop(0, slots // 8, clear, 0)
    for copy in p_copies:
        copy.wait()

    def unpack(q, _):
        for x in range(2):
            parts = [p_vmem[q * 2 + x, t] for t in range(3)]
            p_vmem[q * 2 + x, 3, :, :width] = unpack_last(parts, width)
        return 0

    lax.fori_loop(0, at // 2, unpack, 0)
    if first:

        def transpose(q, _):
            for x in range(4):
                block = p_vmem[q, x].T[:width]
                n = x % per_row
                pt[q * (4 // per_row) + x // per_row, n * width : (n + 1) * width, :] = block
            return 0

        lax.fori_loop(0, at, transpose, 0)
    scale = divider(rows, members)

    def p_block(v):
        j = col_ref[jnp.maximum((v >> 5) - 1, 0), v & 31]
        member = (j * scale) >> 16
        place = ((member ^ me) - cfg["from"]) * rows + j - member * rows
        return jnp.where(v > 0, place, 0)

    def first_product(g, u):
        w = list_ref[phase, g * UNROLL + u]
        j = p_block(w)
        right = jnp.concatenate(
            [p_vmem[j >> 1, (j & 1) * 2 + m] for m in range(per_row)], axis=1
        )
        left = a_rows[(w >> 5) * nonzeros + (w & 31)]
        return jnp.dot(left, right, preferred_element_type=jnp.float32)

    def second_product(u, i):
        return jnp.dot(pt[i], aps[u][...], preferred_element_type=jnp.float32)

    def entry(g, u):
        v = list_ref[phase, g * UNROLL + u]
        return jnp.maximum((v >> 5) - 1, 0), v & 31

    def keep(u, ap):
        aps[u][...] = ap.astype(jnp.bfloat16)

    def collect(i, k, partial):
        for n in range(per_row):
            for m in range(per_row):
                s = tgt_ref[i, n * nonzeros * per_row + k * per_row + m]
                acc[s] = acc[s] + partial[
                    n * width : (n + 1) * width, m * LANES : (m + 1) * LANES
                ]

    def rows_for(g, ready):
        v = list_ref[phase, (g + 1) * UNROLL - 1]
        whole = divider(CHUNK, rows // CHUNK + 1)
        need = jnp.where(v > 0, ((v >> 5) + CHUNK - 1) * whole >> 16, chunks)
        lax.fori_loop(ready, need, wait_chunk, 0)
        return jnp.maximum(ready, need)

    def turn(carry):
        g, ready = carry
        ready = rows_for(g + 1, ready)
        held = None
        for u in range(UNROLL):
            i, k = entry(g, u)
            made = u, i, k, second_product(u, i), first_product(g + 1, u)
            if held is not None:
                keep(held[0], held[4])
                collect(*held[1:4])
            held = made
        keep(held[0], held[4])
        collect(*held[1:4])
        return g + 1, ready

    ready = rows_for(0, jnp.int32(0))
    for u in range(UNROLL):
        keep(u, first_product(0, u))
    g, ready = lax.while_loop(
        lambda c: list_ref[phase, (c[0] + 1) * UNROLL] > 0, turn, (jnp.int32(0), ready)
    )
    for u in range(UNROLL):
        i, k = entry(g, u)
        collect(i, k, second_product(u, i))
    lax.fori_loop(ready, chunks, wait_chunk, 0)
    if last:
        (stage,), (out,) = stages, give_out

        def emit(rz, _):
            pack_part(cfg, acc, stage, rz, 1)
            pltpu.make_async_copy(stage.at[rz], out.at[rz], out_sem.at[0]).start()
            return 0

        lax.fori_loop(0, groups // 2, emit, 0)
        pltpu.make_async_copy(stage, out, out_sem.at[0]).wait()


def pack_part(cfg, acc, to, rz, rc):
    members = cfg["members"]
    me = lax.axis_index("blk").astype(jnp.int32)
    rank = lax.axis_index("grp").astype(jnp.int32)
    group = ((rank >> 1) ^ rz) * 2 + ((rank & 1) ^ rc)
    for r in range(members):
        s = group * (OWN * members) + (me ^ r) * OWN
        packed = pack_four([acc[s + x] for x in range(OWN)], cfg["width"])
        for t in range(3):
            to[rz, r, t] = packed[t].astype(to.dtype)


def keep_kernel(cfg, _, keep_ref, acc):
    def emit(rz, _):
        pack_part(cfg, acc, keep_ref, rz, 0)
        return 0

    lax.fori_loop(0, cfg["groups"] // 2, emit, 0)


def keep_part(cfg, acc):
    vmem = pl.BlockSpec(memory_space=pltpu.VMEM)
    keep, _ = pl.pallas_call(
        functools.partial(keep_kernel, cfg),
        in_specs=[vmem],
        out_specs=[vmem] * 2,
        out_shape=[
            pltpu.VMEM((cfg["groups"] // 2, cfg["members"], 3, cfg["width"], LANES), jnp.float32),
            pltpu.VMEM(acc.shape, acc.dtype),
        ],
        input_output_aliases={0: 1},
        compiler_params=pltpu.CompilerParams(vmem_limit_bytes=8 * 1024 * 1024),
        cost_estimate=pl.CostEstimate(flops=4_000_000, bytes_accessed=4_000_000, transcendentals=0),
        name="keep_part",
    )(acc)
    return keep


def work(cfg, tables, a_rows, packed, acc=None, pt=None):
    width, rows, nonzeros, per_row = cfg["width"], cfg["rows"], cfg["nonzeros"], cfg["per_row"]
    slots, members, groups = cfg["slots"], cfg["members"], cfg["groups"]
    first, last = cfg["first"], cfg["last"]
    cfg = dict(cfg, sources=len(packed))
    quads = sum(x.shape[0] for x in packed)
    vmem = pl.BlockSpec(memory_space=pltpu.VMEM)
    operands = [a_rows.reshape(rows * nonzeros, width, width), *packed]
    in_specs, out_specs = [HBM] * len(operands), [vmem] * 2
    shapes, stages, aliases = [
        pltpu.VMEM((slots, width, LANES), jnp.float32),
        pltpu.VMEM((rows, per_row * width, width), jnp.bfloat16),
    ], [], {}
    resident = slots * width * LANES * 4 + rows * per_row * width * LANES * 2
    if not first:
        operands += [acc, pt]
        in_specs += [vmem] * 2
    if last:
        whole = (groups // 2, members, 3, width, LANES)
        stages = [pltpu.VMEM(whole, jnp.bfloat16)]
        shapes, out_specs = [jax.ShapeDtypeStruct(whole, jnp.bfloat16)] + shapes, [HBM] + out_specs
    if not first:
        aliases = {len(tables) + len(operands) - x: len(shapes) - x for x in (1, 2)}
    return pl.pallas_call(
        functools.partial(work_kernel, cfg),
        grid_spec=pltpu.PrefetchScalarGridSpec(
            num_scalar_prefetch=len(tables),
            grid=(),
            in_specs=in_specs,
            out_specs=out_specs,
            scratch_shapes=[
                pltpu.VMEM((quads, 4, width, LANES), jnp.bfloat16),
                pltpu.VMEM(((rows + 1) * nonzeros, width, width), jnp.bfloat16),
            ]
            + [pltpu.VMEM((width, per_row * LANES), jnp.bfloat16)] * UNROLL
            + [
                pltpu.SemaphoreType.DMA((rows // CHUNK,)),
                pltpu.SemaphoreType.DMA((len(packed),)),
                pltpu.SemaphoreType.DMA((1,)),
            ]
            + stages,
        ),
        out_shape=shapes,
        input_output_aliases=aliases,
        compiler_params=pltpu.CompilerParams(vmem_limit_bytes=VMEM - resident - 256 * 1024),
        cost_estimate=pl.CostEstimate(
            flops=4 * rows * nonzeros * width * width * width,
            bytes_accessed=20_000_000,
            transcendentals=0,
        ),
        name="work_%d" % cfg["phase"],
    )(*tables, *operands)


def make_lists(columns, me, phase_of):
    rows, nonzeros = columns.shape
    entries = rows * nonzeros
    phases = max(phase_of) + 1
    list_len = (-(-entries // UNROLL) + 1) * UNROLL
    relative = ((columns * divider(rows, lax.axis_size("blk"))) >> 16) ^ me
    flat = sum(jnp.where(relative == r, p, 0) for r, p in enumerate(phase_of)).reshape(-1)
    order = jnp.arange(entries, dtype=jnp.int32)
    before = (flat[None, :] == flat[:, None]) & (order[None, :] < order[:, None])
    position = flat * list_len + jnp.sum(before.astype(jnp.int32), axis=1)
    value = (order // nonzeros + 1) * 32 + order % nonzeros
    x = jnp.arange(phases * list_len, dtype=jnp.int32).reshape(phases, list_len)
    found = jnp.where(position[:, None, None] == x[None], value[:, None, None], 0)
    return jnp.sum(found, axis=0)


def shards(a_blocks, col_index, prolong, target):
    rows, nonzeros = a_blocks.shape[1:3]
    per_row = prolong.shape[2]
    width = a_blocks.shape[-1]
    groups = lax.axis_size("grp")
    members = lax.axis_size("blk")
    chips = groups // 2
    slots = groups * OWN * members
    f32, bf16 = jnp.float32, jnp.bfloat16
    me = lax.axis_index("blk").astype(jnp.int32)

    def exchange(x, r, axis="blk", size=members):
        return lax.ppermute(x, axis, [(d, d ^ r) for d in range(size)])

    if members == 4:
        sources = [[0], [1, 2], [3]]
    else:
        sources = [[0]] + [list(range(r, min(r + 3, members))) for r in range(1, members, 3)]
    phases = len(sources)
    phase_of = [p for p in range(phases) for _ in sources[p]]

    own = pack_prolong(prolong)
    direct = range(1, 3 if members == 4 else members)
    packed = {0: own, **{r: [exchange(x, r) for x in own] for r in direct}}
    lists = make_lists(col_index[0], me, phase_of)
    cfg = dict(
        width=width, rows=rows, nonzeros=nonzeros, per_row=per_row, slots=slots,
        members=members, groups=groups,
    )
    acc = pt = None
    for p in range(phases):
        outs = work(
            {**cfg, "phase": p, "first": p == 0, "last": p == phases - 1, "from": sources[p][0]},
            (lists, col_index[0], target[0]), a_blocks[0], [x for r in sources[p] for x in packed[r]], acc, pt,
        )
        acc, pt = outs[-2:]
        if p == 0 and members == 4:
            near, acc = lax.optimization_barrier((packed[1] + packed[2], acc))
            packed = {0: own, 1: near[:2], 2: near[2:]}
            packed[3] = [exchange(near[0], 2), exchange(near[3], 1)]

    given = exchange(outs[0], 1, "grp", groups)
    total = keep_part(cfg, acc) + given.astype(f32)
    got = [exchange(total[:, r].astype(bf16), r) for r in range(1, members)]
    total = total[:, 0]
    for part in got:
        total = total + part.astype(f32)
    got = [exchange(total[r].astype(bf16), 2 * r, "grp", groups) for r in range(1, chips)]
    mine = total[0]
    for part in got:
        mine = mine + part.astype(f32)
    fourth = unpack_last([mine[t] for t in range(3)], width)
    return jnp.concatenate([mine[:, :, :width], fourth[None]])[None]


def solution(mesh):
    return jax.shard_map(
        shards,
        mesh=mesh,
        in_specs=(
            P("grp", "blk", None, None, None),
            P("grp", "blk", None),
            P("grp", "blk", None, None, None),
            P("grp", "blk", None),
        ),
        out_specs=P("grp", "blk", None, None),
        check_vma=False,
    )
```

```python
import functools

import jax
import jax.numpy as jnp
from jax import lax
from jax.experimental import pallas as pl
from jax.experimental.pallas import tpu as pltpu
from jax.sharding import PartitionSpec as P

OWN = 4
UNROLL = 24
LANES = 128
CHUNK = 2
AHEAD = 6
VMEM = 64 * 1024 * 1024
HBM = pl.BlockSpec(memory_space=pl.ANY)


def pack_four(blocks, width):
    strip = LANES - width
    return [
        jnp.concatenate(
            [blocks[t][:, :width], blocks[3][:, strip * t : strip * (t + 1)]], axis=1
        )
        for t in range(3)
    ]


def unpack_last(parts, width):
    return jnp.concatenate([part[:, width:] for part in parts], axis=1)


def pack_kernel(p_hbm, *refs):
    outs, (blocks, packed, in_sem, out_sem) = refs[:2], refs[2:]
    width, quads = p_hbm.shape[-1], p_hbm.shape[0]
    steps = in_sem.shape[0]
    size = quads // steps
    half = steps // 2
    loads, stores = [], []
    for c in range(steps):
        part = pl.ds(c * size, size)
        to = outs[c // half].at[pl.ds(c % half * size, size)]
        loads.append(pltpu.make_async_copy(p_hbm.at[part], blocks.at[part], in_sem.at[c]))
        stores.append(pltpu.make_async_copy(packed.at[part], to, out_sem.at[c]))
        loads[c].start()
    for c in range(steps):
        loads[c].wait()
        for quad in range(c * size, (c + 1) * size):
            made = pack_four([blocks[quad, t] for t in range(4)], width)
            for t in range(3):
                packed[quad, t] = made[t]
        stores[c].start()
    for store in stores:
        store.wait()


def pack_prolong(prolong):
    width, dtype = prolong.shape[-1], prolong.dtype
    quads = prolong.shape[1] * prolong.shape[2] // 4
    steps = 4
    return pl.pallas_call(
        pack_kernel,
        in_specs=[HBM],
        out_specs=[HBM] * 2,
        out_shape=[jax.ShapeDtypeStruct((quads // 2, 3, width, LANES), dtype)] * 2,
        scratch_shapes=[
            pltpu.VMEM((quads, 4, width, width), dtype),
            pltpu.VMEM((quads, 3, width, LANES), dtype),
            pltpu.SemaphoreType.DMA((steps,)),
            pltpu.SemaphoreType.DMA((steps,)),
        ],
        compiler_params=pltpu.CompilerParams(vmem_limit_bytes=VMEM - 128 * 1024),
        name="pack_prolong",
    )(prolong.reshape(quads, 4, width, width))


def divider(rows, members):
    scale = 65536 // rows + 1
    assert all((x * scale) >> 16 == x // rows for x in range(rows * members))
    return scale


def work_kernel(cfg, *refs):
    first, last, phase = cfg["first"], cfg["last"], cfg["phase"]
    width, rows, nonzeros, per_row = cfg["width"], cfg["rows"], cfg["nonzeros"], cfg["per_row"]
    slots, members, groups = cfg["slots"], cfg["members"], cfg["groups"]
    refs = list(refs)
    take = lambda n: [refs.pop(0) for _ in range(n)]
    list_ref, col_ref, tgt_ref, a_hbm = take(4)
    p_hbm = take(cfg["sources"])
    take(0 if first else 2)
    give_out = take(1 if last else 0)
    acc, pt = take(2)
    p_vmem, a_rows = take(2)
    aps = take(UNROLL)
    a_sem, sem, out_sem = take(3)
    stages = take(1 if last else 0)

    me = lax.axis_index("blk").astype(jnp.int32)

    chunks = rows // CHUNK

    def a_copy(c):
        blocks = CHUNK * nonzeros
        to = a_rows.at[pl.ds(nonzeros + c * blocks, blocks)]
        return pltpu.make_async_copy(a_hbm.at[pl.ds(c * blocks, blocks)], to, a_sem.at[c])

    def start_chunk(c, _):
        a_copy(c).start()
        return 0

    def wait_chunk(c, _):
        a_copy(c).wait()

        @pl.when(c + AHEAD < chunks)
        def _():
            a_copy(c + AHEAD).start()

        return 0

    p_copies, at = [], 0
    for s, source in enumerate(p_hbm):
        to = p_vmem.at[pl.ds(at, source.shape[0]), pl.ds(0, 3)]
        p_copies.append(pltpu.make_async_copy(source, to, sem.at[s]))
        at += source.shape[0]
    for copy in p_copies:
        copy.start()
    lax.fori_loop(0, AHEAD, start_chunk, 0)

    a_rows[0] = jnp.zeros((width, width), a_rows.dtype)
    if first:

        def clear(s, _):
            for x in range(8):
                acc[s * 8 + x] = jnp.zeros((width, LANES), acc.dtype)
            return 0

        lax.fori_loop(0, slots // 8, clear, 0)
    for copy in p_copies:
        copy.wait()

    def unpack(q, _):
        for x in range(2):
            parts = [p_vmem[q * 2 + x, t] for t in range(3)]
            p_vmem[q * 2 + x, 3, :, :width] = unpack_last(parts, width)
        return 0

    lax.fori_loop(0, at // 2, unpack, 0)
    if first:

        def transpose(q, _):
            for x in range(4):
                block = p_vmem[q, x].T[:width]
                n = x % per_row
                pt[q * (4 // per_row) + x // per_row, n * width : (n + 1) * width, :] = block
            return 0

        lax.fori_loop(0, at, transpose, 0)
    scale = divider(rows, members)

    def p_block(v):
        j = col_ref[jnp.maximum((v >> 5) - 1, 0), v & 31]
        member = (j * scale) >> 16
        place = ((member ^ me) - cfg["from"]) * rows + j - member * rows
        return jnp.where(v > 0, place, 0)

    def first_product(g, u):
        w = list_ref[phase, g * UNROLL + u]
        j = p_block(w)
        right = jnp.concatenate(
            [p_vmem[j >> 1, (j & 1) * 2 + m] for m in range(per_row)], axis=1
        )
        left = a_rows[(w >> 5) * nonzeros + (w & 31)]
        return jnp.dot(left, right, preferred_element_type=jnp.float32)

    def second_product(u, i):
        return jnp.dot(pt[i], aps[u][...], preferred_element_type=jnp.float32)

    def entry(g, u):
        v = list_ref[phase, g * UNROLL + u]
        return jnp.maximum((v >> 5) - 1, 0), v & 31

    def keep(u, ap):
        aps[u][...] = ap.astype(jnp.bfloat16)

    def collect(i, k, partial):
        for n in range(per_row):
            for m in range(per_row):
                s = tgt_ref[i, n * nonzeros * per_row + k * per_row + m]
                acc[s] = acc[s] + partial[
                    n * width : (n + 1) * width, m * LANES : (m + 1) * LANES
                ]

    def rows_for(g, ready):
        v = list_ref[phase, (g + 1) * UNROLL - 1]
        whole = divider(CHUNK, rows // CHUNK + 1)
        need = jnp.where(v > 0, ((v >> 5) + CHUNK - 1) * whole >> 16, chunks)
        lax.fori_loop(ready, need, wait_chunk, 0)
        return jnp.maximum(ready, need)

    def turn(carry):
        g, ready = carry
        ready = rows_for(g + 1, ready)
        held = None
        for u in range(UNROLL):
            i, k = entry(g, u)
            made = u, i, k, second_product(u, i), first_product(g + 1, u)
            if held is not None:
                keep(held[0], held[4])
                collect(*held[1:4])
            held = made
        keep(held[0], held[4])
        collect(*held[1:4])
        return g + 1, ready

    ready = rows_for(0, jnp.int32(0))
    for u in range(UNROLL):
        keep(u, first_product(0, u))
    g, ready = lax.while_loop(
        lambda c: list_ref[phase, (c[0] + 1) * UNROLL] > 0, turn, (jnp.int32(0), ready)
    )
    for u in range(UNROLL):
        i, k = entry(g, u)
        collect(i, k, second_product(u, i))
    lax.fori_loop(ready, chunks, wait_chunk, 0)
    if last:
        (stage,), (out,) = stages, give_out

        def emit(rz, _):
            pack_part(cfg, acc, stage, rz, 1)
            pltpu.make_async_copy(stage.at[rz], out.at[rz], out_sem.at[0]).start()
            return 0

        lax.fori_loop(0, groups // 2, emit, 0)
        pltpu.make_async_copy(stage, out, out_sem.at[0]).wait()


def pack_part(cfg, acc, to, rz, rc):
    members = cfg["members"]
    me = lax.axis_index("blk").astype(jnp.int32)
    rank = lax.axis_index("grp").astype(jnp.int32)
    group = ((rank >> 1) ^ rz) * 2 + ((rank & 1) ^ rc)
    for r in range(members):
        s = group * (OWN * members) + (me ^ r) * OWN
        packed = pack_four([acc[s + x] for x in range(OWN)], cfg["width"])
        for t in range(3):
            to[rz, r, t] = packed[t].astype(to.dtype)


def keep_kernel(cfg, _, keep_ref, acc):
    def emit(rz, _):
        pack_part(cfg, acc, keep_ref, rz, 0)
        return 0

    lax.fori_loop(0, cfg["groups"] // 2, emit, 0)


def keep_part(cfg, acc):
    vmem = pl.BlockSpec(memory_space=pltpu.VMEM)
    keep, _ = pl.pallas_call(
        functools.partial(keep_kernel, cfg),
        in_specs=[vmem],
        out_specs=[vmem] * 2,
        out_shape=[
            pltpu.VMEM((cfg["groups"] // 2, cfg["members"], 3, cfg["width"], LANES), jnp.float32),
            pltpu.VMEM(acc.shape, acc.dtype),
        ],
        input_output_aliases={0: 1},
        compiler_params=pltpu.CompilerParams(vmem_limit_bytes=8 * 1024 * 1024),
        cost_estimate=pl.CostEstimate(flops=4_000_000, bytes_accessed=4_000_000, transcendentals=0),
        name="keep_part",
    )(acc)
    return keep


def work(cfg, tables, a_rows, packed, acc=None, pt=None):
    width, rows, nonzeros, per_row = cfg["width"], cfg["rows"], cfg["nonzeros"], cfg["per_row"]
    slots, members, groups = cfg["slots"], cfg["members"], cfg["groups"]
    first, last = cfg["first"], cfg["last"]
    cfg = dict(cfg, sources=len(packed))
    quads = sum(x.shape[0] for x in packed)
    vmem = pl.BlockSpec(memory_space=pltpu.VMEM)
    operands = [a_rows.reshape(rows * nonzeros, width, width), *packed]
    in_specs, out_specs = [HBM] * len(operands), [vmem] * 2
    shapes, stages, aliases = [
        pltpu.VMEM((slots, width, LANES), jnp.float32),
        pltpu.VMEM((rows, per_row * width, width), jnp.bfloat16),
    ], [], {}
    resident = slots * width * LANES * 4 + rows * per_row * width * LANES * 2
    if not first:
        operands += [acc, pt]
        in_specs += [vmem] * 2
    if last:
        whole = (groups // 2, members, 3, width, LANES)
        stages = [pltpu.VMEM(whole, jnp.bfloat16)]
        shapes, out_specs = [jax.ShapeDtypeStruct(whole, jnp.bfloat16)] + shapes, [HBM] + out_specs
    if not first:
        aliases = {len(tables) + len(operands) - x: len(shapes) - x for x in (1, 2)}
    return pl.pallas_call(
        functools.partial(work_kernel, cfg),
        grid_spec=pltpu.PrefetchScalarGridSpec(
            num_scalar_prefetch=len(tables),
            grid=(),
            in_specs=in_specs,
            out_specs=out_specs,
            scratch_shapes=[
                pltpu.VMEM((quads, 4, width, LANES), jnp.bfloat16),
                pltpu.VMEM(((rows + 1) * nonzeros, width, width), jnp.bfloat16),
            ]
            + [pltpu.VMEM((width, per_row * LANES), jnp.bfloat16)] * UNROLL
            + [
                pltpu.SemaphoreType.DMA((rows // CHUNK,)),
                pltpu.SemaphoreType.DMA((len(packed),)),
                pltpu.SemaphoreType.DMA((1,)),
            ]
            + stages,
        ),
        out_shape=shapes,
        input_output_aliases=aliases,
        compiler_params=pltpu.CompilerParams(vmem_limit_bytes=VMEM - resident - 256 * 1024),
        cost_estimate=pl.CostEstimate(
            flops=4 * rows * nonzeros * width * width * width,
            bytes_accessed=20_000_000,
            transcendentals=0,
        ),
        name="work_%d" % cfg["phase"],
    )(*tables, *operands)


def make_lists(columns, me, phase_of):
    rows, nonzeros = columns.shape
    entries = rows * nonzeros
    phases = max(phase_of) + 1
    list_len = (-(-entries // UNROLL) + 1) * UNROLL
    relative = ((columns * divider(rows, lax.axis_size("blk"))) >> 16) ^ me
    flat = sum(jnp.where(relative == r, p, 0) for r, p in enumerate(phase_of)).reshape(-1)
    order = jnp.arange(entries, dtype=jnp.int32)
    before = (flat[None, :] == flat[:, None]) & (order[None, :] < order[:, None])
    position = flat * list_len + jnp.sum(before.astype(jnp.int32), axis=1)
    value = (order // nonzeros + 1) * 32 + order % nonzeros
    x = jnp.arange(phases * list_len, dtype=jnp.int32).reshape(phases, list_len)
    found = jnp.where(position[:, None, None] == x[None], value[:, None, None], 0)
    return jnp.sum(found, axis=0)


def shards(a_blocks, col_index, prolong, target):
    rows, nonzeros = a_blocks.shape[1:3]
    per_row = prolong.shape[2]
    width = a_blocks.shape[-1]
    groups = lax.axis_size("grp")
    members = lax.axis_size("blk")
    chips = groups // 2
    slots = groups * OWN * members
    f32, bf16 = jnp.float32, jnp.bfloat16
    me = lax.axis_index("blk").astype(jnp.int32)

    def exchange(x, r, axis="blk", size=members):
        return lax.ppermute(x, axis, [(d, d ^ r) for d in range(size)])

    if members == 4:
        sources = [[0], [1, 2], [3]]
    else:
        sources = [[0]] + [list(range(r, min(r + 3, members))) for r in range(1, members, 3)]
    phases = len(sources)
    phase_of = [p for p in range(phases) for _ in sources[p]]

    own = pack_prolong(prolong)
    direct = range(1, 3 if members == 4 else members)
    packed = {0: own, **{r: [exchange(x, r) for x in own] for r in direct}}
    lists = make_lists(col_index[0], me, phase_of)
    cfg = dict(
        width=width, rows=rows, nonzeros=nonzeros, per_row=per_row, slots=slots,
        members=members, groups=groups,
    )
    acc = pt = None
    for p in range(phases):
        outs = work(
            {**cfg, "phase": p, "first": p == 0, "last": p == phases - 1, "from": sources[p][0]},
            (lists, col_index[0], target[0]), a_blocks[0], [x for r in sources[p] for x in packed[r]], acc, pt,
        )
        acc, pt = outs[-2:]
        if p == 0 and members == 4:
            near, acc = lax.optimization_barrier((packed[1] + packed[2], acc))
            packed = {0: own, 1: near[:2], 2: near[2:]}
            packed[3] = [exchange(near[0], 2), exchange(near[3], 1)]

    given = exchange(outs[0], 1, "grp", groups)
    total = keep_part(cfg, acc) + given.astype(f32)
    got = [exchange(total[:, r].astype(bf16), r) for r in range(1, members)]
    total = total[:, 0]
    for part in got:
        total = total + part.astype(f32)
    got = [exchange(total[r].astype(bf16), 2 * r, "grp", groups) for r in range(1, chips)]
    mine = total[0]
    for part in got:
        mine = mine + part.astype(f32)
    fourth = unpack_last([mine[t] for t in range(3)], width)
    return jnp.concatenate([mine[:, :, :width], fourth[None]])[None]


def solution(mesh):
    return jax.shard_map(
        shards,
        mesh=mesh,
        in_specs=(
            P("grp", "blk", None, None, None),
            P("grp", "blk", None),
            P("grp", "blk", None, None, None),
            P("grp", "blk", None),
        ),
        out_specs=P("grp", "blk", None, None),
        check_vma=False,
    )
```

```python
import functools

import jax
import jax.numpy as jnp
from jax import lax
from jax.experimental import pallas as pl
from jax.experimental.pallas import tpu as pltpu
from jax.sharding import PartitionSpec as P

OWN = 4
UNROLL = 24
LANES = 128
CHUNK = 2
AHEAD = 6
VMEM = 64 * 1024 * 1024
HBM = pl.BlockSpec(memory_space=pl.ANY)


def pack_four(blocks, width):
    strip = LANES - width
    return [
        jnp.concatenate(
            [blocks[t][:, :width], blocks[3][:, strip * t : strip * (t + 1)]], axis=1
        )
        for t in range(3)
    ]


def unpack_last(parts, width):
    return jnp.concatenate([part[:, width:] for part in parts], axis=1)


def pack_kernel(p_hbm, *refs):
    outs, (blocks, packed, in_sem, out_sem) = refs[:2], refs[2:]
    width, quads = p_hbm.shape[-1], p_hbm.shape[0]
    steps = in_sem.shape[0]
    size = quads // steps
    half = steps // 2
    loads, stores = [], []
    for c in range(steps):
        part = pl.ds(c * size, size)
        to = outs[c // half].at[pl.ds(c % half * size, size)]
        loads.append(pltpu.make_async_copy(p_hbm.at[part], blocks.at[part], in_sem.at[c]))
        stores.append(pltpu.make_async_copy(packed.at[part], to, out_sem.at[c]))
        loads[c].start()
    for c in range(steps):
        loads[c].wait()
        for quad in range(c * size, (c + 1) * size):
            made = pack_four([blocks[quad, t] for t in range(4)], width)
            for t in range(3):
                packed[quad, t] = made[t]
        stores[c].start()
    for store in stores:
        store.wait()


def pack_prolong(prolong):
    width, dtype = prolong.shape[-1], prolong.dtype
    quads = prolong.shape[1] * prolong.shape[2] // 4
    steps = 4
    return pl.pallas_call(
        pack_kernel,
        in_specs=[HBM],
        out_specs=[HBM] * 2,
        out_shape=[jax.ShapeDtypeStruct((quads // 2, 3, width, LANES), dtype)] * 2,
        scratch_shapes=[
            pltpu.VMEM((quads, 4, width, width), dtype),
            pltpu.VMEM((quads, 3, width, LANES), dtype),
            pltpu.SemaphoreType.DMA((steps,)),
            pltpu.SemaphoreType.DMA((steps,)),
        ],
        compiler_params=pltpu.CompilerParams(vmem_limit_bytes=VMEM - 128 * 1024),
        name="pack_prolong",
    )(prolong.reshape(quads, 4, width, width))


def divider(rows, members):
    scale = 65536 // rows + 1
    assert all((x * scale) >> 16 == x // rows for x in range(rows * members))
    return scale


def work_kernel(cfg, *refs):
    first, last, phase = cfg["first"], cfg["last"], cfg["phase"]
    width, rows, nonzeros, per_row = cfg["width"], cfg["rows"], cfg["nonzeros"], cfg["per_row"]
    slots, members, groups = cfg["slots"], cfg["members"], cfg["groups"]
    refs = list(refs)
    take = lambda n: [refs.pop(0) for _ in range(n)]
    list_ref, col_ref, tgt_ref, a_hbm = take(4)
    p_hbm = take(cfg["sources"])
    naccs = cfg["naccs"]
    take(0 if first else naccs + 1)
    give_out = take(1 if last else 0)
    accs = take(naccs)
    (pt,) = take(1)
    p_vmem, a_rows = take(2)
    aps = take(UNROLL)
    a_sem, sem, out_sem = take(3)
    stages = take(1 if last else 0)

    me = lax.axis_index("blk").astype(jnp.int32)

    chunks = rows // CHUNK

    def a_copy(c):
        blocks = CHUNK * nonzeros
        to = a_rows.at[pl.ds(nonzeros + c * blocks, blocks)]
        return pltpu.make_async_copy(a_hbm.at[pl.ds(c * blocks, blocks)], to, a_sem.at[c])

    def start_chunk(c, _):
        a_copy(c).start()
        return 0

    def wait_chunk(c, _):
        a_copy(c).wait()

        @pl.when(c + AHEAD < chunks)
        def _():
            a_copy(c + AHEAD).start()

        return 0

    p_copies, at = [], 0
    for s, source in enumerate(p_hbm):
        to = p_vmem.at[pl.ds(at, source.shape[0]), pl.ds(0, 3)]
        p_copies.append(pltpu.make_async_copy(source, to, sem.at[s]))
        at += source.shape[0]
    for copy in p_copies:
        copy.start()
    lax.fori_loop(0, AHEAD, start_chunk, 0)

    a_rows[0] = jnp.zeros((width, width), a_rows.dtype)
    if first:

        def clear(s, _):
            for x in range(8):
                for acc in accs:
                    acc[s * 8 + x] = jnp.zeros((width, LANES), acc.dtype)
            return 0

        lax.fori_loop(0, slots // 8, clear, 0)
    for copy in p_copies:
        copy.wait()

    def unpack(q, _):
        for x in range(2):
            parts = [p_vmem[q * 2 + x, t] for t in range(3)]
            p_vmem[q * 2 + x, 3, :, :width] = unpack_last(parts, width)
        return 0

    lax.fori_loop(0, at // 2, unpack, 0)
    if first:

        def transpose(q, _):
            for x in range(4):
                block = p_vmem[q, x].T[:width]
                n = x % per_row
                pt[q * (4 // per_row) + x // per_row, n * width : (n + 1) * width, :] = block
            return 0

        lax.fori_loop(0, at, transpose, 0)
    scale = divider(rows, members)

    def p_block(v):
        j = col_ref[jnp.maximum((v >> 5) - 1, 0), v & 31]
        member = (j * scale) >> 16
        place = ((member ^ me) - cfg["from"]) * rows + j - member * rows
        return jnp.where(v > 0, place, 0)

    def first_product(g, u):
        w = list_ref[phase, g * UNROLL + u]
        j = p_block(w)
        right = jnp.concatenate(
            [p_vmem[j >> 1, (j & 1) * 2 + m] for m in range(per_row)], axis=1
        )
        left = a_rows[(w >> 5) * nonzeros + (w & 31)]
        return jnp.dot(left, right, preferred_element_type=jnp.float32)

    def second_product(u, i):
        return jnp.dot(pt[i], aps[u][...], preferred_element_type=jnp.float32)

    def entry(g, u):
        v = list_ref[phase, g * UNROLL + u]
        return jnp.maximum((v >> 5) - 1, 0), v & 31

    def keep(u, ap):
        aps[u][...] = ap.astype(jnp.bfloat16)

    def collect(i, k, partial):
        for n in range(per_row):
            for m in range(per_row):
                acc = accs[m % naccs]
                s = tgt_ref[i, n * nonzeros * per_row + k * per_row + m]
                acc[s] = acc[s] + partial[
                    n * width : (n + 1) * width, m * LANES : (m + 1) * LANES
                ]

    def rows_for(g, ready):
        v = list_ref[phase, (g + 1) * UNROLL - 1]
        whole = divider(CHUNK, rows // CHUNK + 1)
        need = jnp.where(v > 0, ((v >> 5) + CHUNK - 1) * whole >> 16, chunks)
        lax.fori_loop(ready, need, wait_chunk, 0)
        return jnp.maximum(ready, need)

    def turn(carry):
        g, ready = carry
        ready = rows_for(g + 1, ready)
        held = None
        for u in range(UNROLL):
            i, k = entry(g, u)
            made = u, i, k, second_product(u, i), first_product(g + 1, u)
            if held is not None:
                keep(held[0], held[4])
                collect(*held[1:4])
            held = made
        keep(held[0], held[4])
        collect(*held[1:4])
        return g + 1, ready

    ready = rows_for(0, jnp.int32(0))
    for u in range(UNROLL):
        keep(u, first_product(0, u))
    g, ready = lax.while_loop(
        lambda c: list_ref[phase, (c[0] + 1) * UNROLL] > 0, turn, (jnp.int32(0), ready)
    )
    for u in range(UNROLL):
        i, k = entry(g, u)
        collect(i, k, second_product(u, i))
    lax.fori_loop(ready, chunks, wait_chunk, 0)
    if last:
        (stage,), (out,) = stages, give_out

        def emit(rz, _):
            pack_part(cfg, accs, stage, rz, 1)
            pltpu.make_async_copy(stage.at[rz], out.at[rz], out_sem.at[0]).start()
            return 0

        lax.fori_loop(0, groups // 2, emit, 0)
        pltpu.make_async_copy(stage, out, out_sem.at[0]).wait()


def pack_part(cfg, accs, to, rz, rc):
    members = cfg["members"]
    me = lax.axis_index("blk").astype(jnp.int32)
    rank = lax.axis_index("grp").astype(jnp.int32)
    group = ((rank >> 1) ^ rz) * 2 + ((rank & 1) ^ rc)
    for r in range(members):
        s = group * (OWN * members) + (me ^ r) * OWN
        packed = pack_four([sum(acc[s + x] for acc in accs) for x in range(OWN)], cfg["width"])
        for t in range(3):
            to[rz, r, t] = packed[t].astype(to.dtype)


def keep_kernel(cfg, *refs):
    keep_ref, *accs = refs[cfg["naccs"] :]

    def emit(rz, _):
        pack_part(cfg, accs, keep_ref, rz, 0)
        return 0

    lax.fori_loop(0, cfg["groups"] // 2, emit, 0)


def keep_part(cfg, accs):
    vmem = pl.BlockSpec(memory_space=pltpu.VMEM)
    return pl.pallas_call(
        functools.partial(keep_kernel, cfg),
        in_specs=[vmem] * len(accs),
        out_specs=[vmem] * (1 + len(accs)),
        out_shape=[
            pltpu.VMEM((cfg["groups"] // 2, cfg["members"], 3, cfg["width"], LANES), jnp.float32),
            *[pltpu.VMEM(acc.shape, acc.dtype) for acc in accs],
        ],
        input_output_aliases={x: x + 1 for x in range(len(accs))},
        compiler_params=pltpu.CompilerParams(vmem_limit_bytes=8 * 1024 * 1024),
        cost_estimate=pl.CostEstimate(flops=4_000_000, bytes_accessed=4_000_000, transcendentals=0),
        name="keep_part",
    )(*accs)[0]


def work(cfg, tables, a_rows, packed, accs=None, pt=None):
    width, rows, nonzeros, per_row = cfg["width"], cfg["rows"], cfg["nonzeros"], cfg["per_row"]
    slots, members, groups = cfg["slots"], cfg["members"], cfg["groups"]
    first, last = cfg["first"], cfg["last"]
    cfg = dict(cfg, sources=len(packed))
    quads = sum(x.shape[0] for x in packed)
    vmem = pl.BlockSpec(memory_space=pltpu.VMEM)
    operands = [a_rows.reshape(rows * nonzeros, width, width), *packed]
    in_specs, out_specs = [HBM] * len(operands), [vmem] * (cfg["naccs"] + 1)
    shapes, stages, aliases = [
        *[pltpu.VMEM((slots, width, LANES), jnp.float32)] * cfg["naccs"],
        pltpu.VMEM((rows, per_row * width, width), jnp.bfloat16),
    ], [], {}
    resident = cfg["naccs"] * slots * width * LANES * 4 + rows * per_row * width * LANES * 2
    if not first:
        operands += [*accs, pt]
        in_specs += [vmem] * (cfg["naccs"] + 1)
    if last:
        whole = (groups // 2, members, 3, width, LANES)
        stages = [pltpu.VMEM(whole, jnp.bfloat16)]
        shapes, out_specs = [jax.ShapeDtypeStruct(whole, jnp.bfloat16)] + shapes, [HBM] + out_specs
    if not first:
        aliases = {len(tables) + len(operands) - x: len(shapes) - x for x in range(1, cfg["naccs"] + 2)}
    return pl.pallas_call(
        functools.partial(work_kernel, cfg),
        grid_spec=pltpu.PrefetchScalarGridSpec(
            num_scalar_prefetch=len(tables),
            grid=(),
            in_specs=in_specs,
            out_specs=out_specs,
            scratch_shapes=[
                pltpu.VMEM((quads, 4, width, LANES), jnp.bfloat16),
                pltpu.VMEM(((rows + 1) * nonzeros, width, width), jnp.bfloat16),
            ]
            + [pltpu.VMEM((width, per_row * LANES), jnp.bfloat16)] * UNROLL
            + [
                pltpu.SemaphoreType.DMA((rows // CHUNK,)),
                pltpu.SemaphoreType.DMA((len(packed),)),
                pltpu.SemaphoreType.DMA((1,)),
            ]
            + stages,
        ),
        out_shape=shapes,
        input_output_aliases=aliases,
        compiler_params=pltpu.CompilerParams(vmem_limit_bytes=VMEM - resident - 256 * 1024),
        cost_estimate=pl.CostEstimate(
            flops=4 * rows * nonzeros * width * width * width,
            bytes_accessed=20_000_000,
            transcendentals=0,
        ),
        name="work_%d" % cfg["phase"],
    )(*tables, *operands)


def make_lists(columns, me, phase_of):
    rows, nonzeros = columns.shape
    entries = rows * nonzeros
    phases = max(phase_of) + 1
    list_len = (-(-entries // UNROLL) + 1) * UNROLL
    relative = ((columns * divider(rows, lax.axis_size("blk"))) >> 16) ^ me
    flat = sum(jnp.where(relative == r, p, 0) for r, p in enumerate(phase_of)).reshape(-1)
    order = jnp.arange(entries, dtype=jnp.int32)
    before = (flat[None, :] == flat[:, None]) & (order[None, :] < order[:, None])
    position = flat * list_len + jnp.sum(before.astype(jnp.int32), axis=1)
    value = (order // nonzeros + 1) * 32 + order % nonzeros
    x = jnp.arange(phases * list_len, dtype=jnp.int32).reshape(phases, list_len)
    found = jnp.where(position[:, None, None] == x[None], value[:, None, None], 0)
    return jnp.sum(found, axis=0)


def shards(a_blocks, col_index, prolong, target):
    rows, nonzeros = a_blocks.shape[1:3]
    per_row = prolong.shape[2]
    width = a_blocks.shape[-1]
    groups = lax.axis_size("grp")
    members = lax.axis_size("blk")
    chips = groups // 2
    slots = groups * OWN * members
    f32, bf16 = jnp.float32, jnp.bfloat16
    me = lax.axis_index("blk").astype(jnp.int32)

    def exchange(x, r, axis="blk", size=members):
        return lax.ppermute(x, axis, [(d, d ^ r) for d in range(size)])

    if members == 4:
        sources = [[0], [1, 2], [3]]
    else:
        sources = [[0]] + [list(range(r, min(r + 3, members))) for r in range(1, members, 3)]
    phases = len(sources)
    phase_of = [p for p in range(phases) for _ in sources[p]]

    own = pack_prolong(prolong)
    direct = range(1, 3 if members == 4 else members)
    packed = {0: own, **{r: [exchange(x, r) for x in own] for r in direct}}
    lists = make_lists(col_index[0], me, phase_of)
    cfg = dict(
        width=width, rows=rows, nonzeros=nonzeros, per_row=per_row, slots=slots,
        members=members, groups=groups,
        naccs=2 if slots <= 128 else 1,
    )
    accs = pt = None
    for p in range(phases):
        outs = work(
            {**cfg, "phase": p, "first": p == 0, "last": p == phases - 1, "from": sources[p][0]},
            (lists, col_index[0], target[0]), a_blocks[0], [x for r in sources[p] for x in packed[r]], accs, pt,
        )
        accs, pt = outs[-1 - cfg["naccs"] : -1], outs[-1]
        if p == 0 and members == 4:
            near, accs = lax.optimization_barrier((packed[1] + packed[2], accs))
            packed = {0: own, 1: near[:2], 2: near[2:]}
            packed[3] = [exchange(near[0], 2), exchange(near[3], 1)]

    given = exchange(outs[0], 1, "grp", groups)
    total = keep_part(cfg, accs) + given.astype(f32)
    got = [exchange(total[:, r].astype(bf16), r) for r in range(1, members)]
    total = total[:, 0]
    for part in got:
        total = total + part.astype(f32)
    got = [exchange(total[r].astype(bf16), 2 * r, "grp", groups) for r in range(1, chips)]
    mine = total[0]
    for part in got:
        mine = mine + part.astype(f32)
    fourth = unpack_last([mine[t] for t in range(3)], width)
    return jnp.concatenate([mine[:, :, :width], fourth[None]])[None]


def solution(mesh):
    return jax.shard_map(
        shards,
        mesh=mesh,
        in_specs=(
            P("grp", "blk", None, None, None),
            P("grp", "blk", None),
            P("grp", "blk", None, None, None),
            P("grp", "blk", None),
        ),
        out_specs=P("grp", "blk", None, None),
        check_vma=False,
    )
```
